512 devices in a mesh: dp: 64 (over z, y), enc: 8 (over x, core).
Axes of the slice: x: 4, y: 4, z: 16, core: 2. Of those that a mesh axis runs over, the one named last changes fastest.
Arguments:
- tile_features: bfloat16 [4096, 4, 2, 3072], P('dp', None, None, 'enc'), may hold values from -6 to 6
- dw_kernel: float32 [49, 3072], P(None, 'enc'), may hold values from -0.875 to 0.875
- dw_bias: float32 [3072], P('enc'), may hold values from -3 to 3
- ln_gain: float32 [3072], P('enc'), may hold values from 0.1 to 1.9
- ln_shift: float32 [3072], P('enc'), may hold values from -3 to 3
- layer_scale: float32 [3072], P('enc'), may hold values from 0.3 to 3
- sample_counts: int32 [64, 8], P('dp'), may hold values from 1 to 16, 64 in all within a row
- tile_dest: int32 [64, 64], P('dp'), may hold values from 0 to 63, as said below
- tile_offset: int32 [64, 64], P('dp'), may hold values from 0 to 127, as said below
- seq_grad: bfloat16 [65536, 3072], P('dp', 'enc'), may hold values from -6 to 6
Outputs:
- visual_sequence: bfloat16 [65536, 3072], P('dp', 'enc')
- tile_grads: bfloat16 [4096, 4, 2, 3072], P('dp', None, None, 'enc')
- param_grads: float32 [53, 3072], P(None, 'enc')
The draws below stay inside these ranges and needn't reach their ends.
Inputs may be any that keep to these rules, and one draw needn't show every extreme that they name: `tile_dest`: among one owner's tiles each shard is named at most 2 times; in every draw some shard is named exactly 2 times by every owner, so its 128 blocks are all used. `tile_offset`: tiles sent to one shard have distinct blocks. `sample_counts`: the counts of one owner sum to 64; the largest is 16.
All inputs are finite; a program needn't handle non-finite values.
Results may differ from the reference program's by a relative error of at most 0.00105.
Values may be sent and summed in bfloat16 or wider, within the bound.
No kernel may reach another device: no remote copies, remote signals or barrier semaphores. Data moves between devices by JAX's collectives and lax.ppermute only.
A program may use at most 64 MiB of HBM per device.

```python
import math
import jax
import jax.numpy as jnp
import numpy as np
from jax import lax

C = 3072
TH = 4
TW = 2
TILES_DEV = 64
MAXT = 16
S_DEV = 8
CAP = 2
BLOCKS = 128
SEQ_DEV = 1024
TILES = 4096
N_DP = 64


def routing(key):
    base = jax.random.fold_in(key, 101)
    k_pop, k_hot, k_rank, k_shuffle, k_block = jax.random.split(base, 5)
    popular = jax.random.randint(k_pop, (N_DP,), 0, 4)
    popular = popular.at[jax.random.randint(k_hot, (), 0, N_DP)].set(4)
    slot_total = N_DP * CAP
    slot_target = jnp.arange(slot_total, dtype=jnp.int32) // CAP
    order = jax.vmap(lambda k: jax.random.permutation(k, slot_total))(jax.random.split(k_rank, N_DP))
    score = popular[slot_target][None, :] * (1 << 20) + order.astype(jnp.int32)
    chosen = lax.top_k(score, TILES_DEV)[1].astype(jnp.int32)
    targets = chosen // CAP
    mixing = jax.vmap(lambda k: jax.random.permutation(k, TILES_DEV))(jax.random.split(k_shuffle, N_DP))
    targets = jnp.take_along_axis(targets, mixing.astype(jnp.int32), 1)
    flat = targets.reshape(-1)
    picks = (flat[:, None] == jnp.arange(N_DP, dtype=jnp.int32)[None, :]).astype(jnp.int32)
    rank = jnp.sum((jnp.cumsum(picks, 0) - 1) * picks, 1)
    layout = jax.vmap(lambda k: jax.random.permutation(k, BLOCKS))(jax.random.split(k_block, N_DP)).astype(jnp.int32)
    offsets = layout[flat, rank].reshape(N_DP, TILES_DEV)
    return (targets.astype(jnp.int32), offsets.astype(jnp.int32))


def draw_tile_dest(key, part):
    return routing(key)[0]


def draw_tile_offset(key, part):
    return routing(key)[1]


def level_of(own_key, shape, shards, least, high):
    loudness, own = 1.0, jax.random.fold_in(own_key, 6)
    for axis_at, parts in shards:
        heights = jnp.exp(jax.random.uniform(jax.random.fold_in(own, axis_at), (parts,), jnp.float32, least / len(shards), high / len(shards)))
        loudness = loudness * jnp.repeat(heights, shape[axis_at] // parts).reshape([-1 if axis == axis_at else 1 for axis in range(len(shape))])
    return loudness


def split_up(number_of, total, reach, lean):
    weights = [(1 << 20) // math.isqrt(standing ** lean) + 1 for standing in range(2, number_of + 1)]
    rest, holding = total - reach - (number_of - 1), [1] * (number_of - 1)
    while rest > 0:
        candidates = [i for i in range(number_of - 1) if holding[i] < reach]
        pool, budget = sum([weights[i] for i in candidates]), rest
        for i in candidates:
            more = min(reach - holding[i], max(1, budget * weights[i] // pool), rest)
            holding[i] = holding[i] + more
            rest = rest - more
    return np.array([reach] + holding)


def uneven(own_key, amount, total, reach, slope):
    if amount == 2:
        one = jax.random.randint(own_key, (), max(1, total - reach), min(reach, total - 1) + 1)
        return jnp.stack([one, total - one])
    sizes = jnp.asarray(split_up(amount, total, reach, slope), jnp.int32)
    couples = (amount - 1) // 2
    giver, taker = sizes[1:1 + 2 * couples:2], sizes[2:2 + 2 * couples:2]
    slack = jnp.minimum(giver - 1, reach - taker)
    passed = jax.random.randint(jax.random.fold_in(own_key, 1), (couples,), 0, 1 << 20) % (slack + 1)
    sizes = sizes.at[1:1 + 2 * couples:2].set(giver - passed).at[2:2 + 2 * couples:2].set(taker + passed)
    return sizes[jax.random.permutation(jax.random.fold_in(own_key, 2), amount)]


def noise(key, extent, scale, most, cuts=(), held_as=jnp.bfloat16):
    drawn = scale * jax.random.normal(key, extent, jnp.float32)
    if cuts:
        drawn = drawn * level_of(key, extent, cuts, -0.22, 0.18)
    return jnp.clip(drawn, -most, most).astype(held_as)


def setup_inputs(seed: int = 0) -> dict:
    streams_of = jax.random.split(jax.random.key(seed), 11)
    tile_features = noise(streams_of[0], (TILES, TH, TW, C), 1.0, 6.0, ((0, 64), (3, 8)))
    dw_kernel = noise(streams_of[1], (49, C), 49 ** -0.5, 0.875, ((1, 8),), jnp.float32)
    dw_bias = noise(streams_of[2], (C,), 0.5, 3.0, ((0, 8),), jnp.float32)
    ln_gain = jnp.clip(1.0 + 0.18 * jax.random.normal(streams_of[3], (C,), jnp.float32), 0.1, 1.9)
    ln_shift = noise(streams_of[4], (C,), 0.5, 3.0, ((0, 8),), jnp.float32)
    layer_scale = jnp.clip(jnp.exp(math.log(3.0) - 2.3025851 * jax.random.uniform(streams_of[5], (C,), jnp.float32) ** level_of(streams_of[5], (C,), ((0, 8),), -0.2, 0.2)), 0.3, 3.0)
    sample_counts = jax.vmap(lambda own: uneven(own, S_DEV, TILES_DEV, MAXT, 2))(jax.random.split(streams_of[6], N_DP)).reshape((N_DP, S_DEV)).astype(jnp.int32)
    tile_dest = draw_tile_dest(jax.random.fold_in(streams_of[10], 71), 0)
    tile_offset = draw_tile_offset(jax.random.fold_in(streams_of[10], 71), 0)
    seq_grad = noise(streams_of[9], (N_DP * SEQ_DEV, C), 1.0, 6.0, ((0, 64), (1, 8)))
    return dict(tile_features=tile_features, dw_kernel=dw_kernel, dw_bias=dw_bias, ln_gain=ln_gain, ln_shift=ln_shift, layer_scale=layer_scale, sample_counts=sample_counts, tile_dest=tile_dest, tile_offset=tile_offset, seq_grad=seq_grad)


EPS = 1e-06

def conv_apply(tiles, kernel):
    hgt, wid = (tiles.shape[1], tiles.shape[2])
    padded = jnp.pad(tiles, ((0, 0), (3, 3), (3, 3), (0, 0)))
    total = jnp.zeros(tiles.shape, jnp.float32)
    for row in range(7):
        for col in range(7):
            total = total + kernel[row * 7 + col] * padded[:, row:row + hgt, col:col + wid, :]
    return total

def block_forward(tiles, kernel, bias, gain, shift, scale):
    filtered = conv_apply(tiles, kernel) + bias
    center = lax.optimization_barrier(jnp.mean(filtered, -1, keepdims=True))
    spread = lax.optimization_barrier(jnp.mean(filtered * filtered, -1, keepdims=True)) - center * center
    normed = (filtered - center) * lax.rsqrt(spread + EPS)
    return tiles + scale * (normed * gain + shift)

def reference(tile_features, dw_kernel, dw_bias, ln_gain, ln_shift, layer_scale, sample_counts, tile_dest, tile_offset, seq_grad):
    ends = jnp.cumsum(sample_counts, 1)
    positions = jnp.arange(TILES_DEV, dtype=jnp.int32)
    sample = lax.optimization_barrier(jnp.sum((positions[None, :, None] >= ends[:, None, :]).astype(jnp.int32), 2))
    tile_count = jnp.take_along_axis(sample_counts, sample, 1)
    weight = 8.0 / tile_count.astype(jnp.float32)
    base = (tile_dest * BLOCKS + tile_offset).reshape(-1).astype(jnp.int32)
    grad_blocks = seq_grad.reshape(N_DP * BLOCKS, TH, TW, C)
    chosen = grad_blocks[base].reshape(N_DP, TILES_DEV, TH, TW, C)
    tiles_all = tile_features.reshape(N_DP, TILES_DEV, TH, TW, C)

    def owner_step(carry, items):
        tiles, rows, wts = items
        primal = tiles.astype(jnp.float32)
        tokens, pullback = jax.vjp(block_forward, primal, dw_kernel, dw_bias, ln_gain, ln_shift, layer_scale)
        upstream = rows.astype(jnp.float32) * wts[:, None, None, None]
        dtiles, dkern, dbias, dgain, dshift, dscale = pullback(upstream)
        grads = jnp.concatenate([dkern, jnp.stack([dbias, dgain, dshift, dscale], 0)], 0)
        return (carry + grads, (tokens.astype(jnp.bfloat16), dtiles.astype(jnp.bfloat16)))
    start = jnp.zeros((53, C), jnp.float32)
    param_grads, outs = lax.scan(owner_step, start, (tiles_all, chosen, weight))
    tokens, dtiles = outs
    placed = jnp.zeros((N_DP * BLOCKS, TH, TW, C), jnp.bfloat16)
    placed = placed.at[base].set(tokens.reshape(TILES, TH, TW, C))
    visual_sequence = placed.reshape(N_DP * SEQ_DEV, C)
    tile_grads = dtiles.reshape(TILES, TH, TW, C)
    return (visual_sequence, tile_grads, param_grads)
```

```python
import functools

import jax
import jax.numpy as jnp
from jax import lax
from jax.experimental import pallas as pl
from jax.experimental.pallas import tpu as pltpu
from jax.sharding import Mesh
from jax.sharding import PartitionSpec as P

EPS = 1e-06
HGT, WID = 4, 2
POS = HGT * WID
LANES = 128
DP = ("zh", "zl", "y")
ENC = ("x", "core")
VMEM_LIMIT = 16 * 1024 * 1024


def full(a, b):
    (ha, wa), (hb, wb) = divmod(a, WID), divmod(b, WID)
    return (hb - ha + 3) * 7 + (wb - wa + 3)


USED = sorted({full(a, b) for a in range(POS) for b in range(POS)})
PLACE = {tap: i for i, tap in enumerate(USED)}
ROWS = len(USED) + 3


def pack_kernel(peers, cap, part, ints_hbm, tiles_ref, send_ref, slot_ref, rows, data, seen, ints, sem):
    fetch = pltpu.make_async_copy(ints_hbm, ints, sem)
    fetch.start()
    tiles = tiles_ref.shape[0] // POS
    cbs = tiles_ref.shape[1] // LANES
    meta = cbs * cap * POS
    data[...] = jnp.zeros_like(data)
    for cb in range(cbs):
        rows[cb] = tiles_ref[:, cb * LANES : (cb + 1) * LANES].astype(jnp.float32)

    def clear(i, c):
        seen[i] = 0
        return c

    lax.fori_loop(0, peers, clear, 0, unroll=8)
    fetch.wait()
    lane = lax.broadcasted_iota(jnp.int32, (1, LANES), 1)

    def move(t, carry):
        s, end = carry
        step = (t >= end).astype(jnp.int32)
        s = s + step
        count = ints[0, 2 * tiles + s]
        end = end + step * count
        d = ints[0, t]
        r = seen[d]
        seen[d] = r + 1
        slot_ref[t] = d * cap + r
        for cb in range(cbs):
            at = d * part + cb * cap * POS + r * POS
            data[pl.ds(at, POS), :] = rows[cb, pl.ds(pl.multiple_of(t * POS, POS), POS), :]
        note = jnp.where(lane == r, ints[0, tiles + t], jnp.where(lane == cap + r, count, 0))
        here = pl.ds(d * part + meta, 1)
        data[here, :] = data[here, :] + note.astype(jnp.float32)
        return s, end

    lax.fori_loop(0, tiles, move, (jnp.int32(0), ints[0, 2 * tiles]), unroll=4)
    send_ref[...] = data[...].astype(jnp.bfloat16)


def conv_kernel(peers, cap, part, got_ref, seq_ref, kern_ref, bias_ref, gain_ref, scale_ref,
                x_ref, u_ref, f_ref, sums_ref, off_ref,
                data, seq, ups, cols, off_v, wgt_v, off_s, wgt_s, sem):
    cbs = seq_ref.shape[1] // LANES
    slots = peers * cap
    blocks = seq_ref.shape[0] // POS
    meta = cbs * cap * POS
    data[...] = got_ref[...].astype(jnp.float32)
    notes = data[pl.ds(meta, peers, stride=part), :]
    notes = jnp.concatenate([notes, jnp.zeros((LANES - peers, LANES), jnp.float32)], 0).T
    count = notes[cap : 2 * cap]
    off_v[0:cap] = jnp.where(count > 0.5, notes[0:cap], float(blocks)).astype(jnp.int32)
    wgt_v[0:cap] = jnp.where(count > 0.5, 8.0 / jnp.maximum(count, 1.0), 0.0)
    moves = [pltpu.make_async_copy(off_v, off_s, sem.at[0]), pltpu.make_async_copy(wgt_v, wgt_s, sem.at[1])]
    for m in moves:
        m.start()
    for cb in range(cbs):
        seq[cb, 0 : blocks * POS, :] = seq_ref[:, cb * LANES : (cb + 1) * LANES].astype(jnp.float32)
        seq[cb, blocks * POS :, :] = jnp.zeros((POS, LANES), jnp.float32)
    for m in moves:
        m.wait()
    for r in range(cap):

        def fetch(d, c, r=r):
            off, w = off_s[r, d], wgt_s[r, d]
            off_ref[r * peers + d] = off
            for cb in range(cbs):
                ups[cb, pl.ds(pl.multiple_of((r * peers + d) * POS, POS), POS), :] = (
                    seq[cb, pl.ds(pl.multiple_of(off * POS, POS), POS), :] * w
                )
            return c

        lax.fori_loop(0, peers, fetch, 0, unroll=8)
    lane = lax.broadcasted_iota(jnp.int32, (8, LANES), 1)
    for r in range(cap):

        def body(b, c, r=r):
            here = pl.ds(pl.multiple_of(r * peers + b * 8, 8), 8)
            xs = {}
            for cb in range(cbs):
                for q in range(POS):
                    x = data[pl.ds(b * 8 * part + cb * cap * POS + r * POS + q, 8, stride=part), :]
                    x_ref[cb, q, here, :] = x
                    xs[cb, q] = x
            out = jnp.zeros((8, LANES), jnp.float32)
            for p in range(POS):
                tot = [None] * 4
                for cb in range(cbs):
                    ch = slice(cb * LANES, (cb + 1) * LANES)
                    f = bias_ref[:, ch] + kern_ref[full(p, 0) : full(p, 0) + 1, ch] * xs[cb, 0]
                    for q in range(1, POS):
                        f = f + kern_ref[full(p, q) : full(p, q) + 1, ch] * xs[cb, q]
                    f_ref[cb, p, here, :] = f
                    u = ups[cb, pl.ds((r * peers + b * 8) * POS + p, 8, stride=POS), :]
                    u_ref[cb, p, here, :] = u
                    dn = u * (scale_ref[:, ch] * gain_ref[:, ch])
                    new = [f, f * f, dn, dn * f]
                    tot = new if cb == 0 else [a + n for a, n in zip(tot, new)]
                for k in range(4):
                    out = jnp.where(lane == k * POS + p, jnp.sum(tot[k], 1, keepdims=True), out)
            cols[here, :] = out
            return c

        lax.fori_loop(0, peers // 8, body, 0)
    total = cols[...].T[0 : 4 * POS]
    for i in range(sums_ref.shape[0]):
        sums_ref[i] = total


def stats_columns(sums_ref, width):
    sums = sums_ref[0]
    for i in range(1, sums_ref.shape[0]):
        sums = sums + sums_ref[i]
    center = sums[0:POS] / width
    inv = lax.rsqrt(jnp.maximum(sums[POS : 2 * POS] / width - center * center, 0.0) + EPS)
    first = sums[2 * POS : 3 * POS]
    second = inv * (sums[3 * POS : 4 * POS] - center * first)
    slots = sums.shape[1]
    rows = [center, inv, first / width, second / width, jnp.zeros((LANES - 4 * POS, slots), jnp.float32)]
    return jnp.concatenate(rows, 0).T


def grad_kernel(peers, cap, width, sums_ref, x_ref, u_ref, f_ref, kern_ref, gain_ref, scale_ref,
                out_ref, part_ref, stats, data, acc):
    cbs = x_ref.shape[0]
    part = cbs * cap * POS
    stats[...] = stats_columns(sums_ref, width)
    acc[...] = jnp.zeros_like(acc)
    for cb in range(cbs):
        ch = slice(cb * LANES, (cb + 1) * LANES)
        for r in range(cap):

            def body(b, c, r=r, cb=cb, ch=ch):
                here = pl.ds(pl.multiple_of(r * peers + b * 8, 8), 8)
                st = stats[here, :]

                def add(row, v):
                    acc[row, :, ch] = acc[row, :, ch] + v

                df, xs, us = [], [], []
                a_sum = b_sum = d_sum = None
                for p in range(POS):
                    col = [st[:, k * POS + p : k * POS + p + 1] for k in range(4)]
                    u = u_ref[cb, p, here, :]
                    n = (f_ref[cb, p, here, :] - col[0]) * col[1]
                    d = col[1] * (u * (scale_ref[:, ch] * gain_ref[:, ch]) - col[2] - n * col[3])
                    df.append(d)
                    us.append(u)
                    xs.append(x_ref[cb, p, here, :])
                    a_sum = u * n if p == 0 else a_sum + u * n
                    b_sum = u if p == 0 else b_sum + u
                    d_sum = d if p == 0 else d_sum + d
                taps = {}
                for p in range(POS):
                    for q in range(POS):
                        t = PLACE[full(p, q)]
                        v = df[p] * xs[q]
                        taps[t] = v if t not in taps else taps[t] + v
                for t, v in taps.items():
                    add(t, v)
                add(len(USED), d_sum)
                add(len(USED) + 1, a_sum)
                add(len(USED) + 2, b_sum)
                for q in range(POS):
                    t = us[q]
                    for p in range(POS):
                        t = t + kern_ref[full(p, q) : full(p, q) + 1, ch] * df[p]
                    data[pl.ds(b * 8 * part + cb * cap * POS + r * POS + q, 8, stride=part), :] = t
                return c

            lax.fori_loop(0, peers // 8, body, 0)
    out_ref[...] = data[...].astype(jnp.bfloat16)
    for row in range(ROWS):
        part_ref[row : row + 1, :] = jnp.sum(acc[row], 0, keepdims=True)


def token_kernel(peers, cap, width, off_ref, sums_ref, x_ref, f_ref, gain_ref, shift_ref, scale_ref,
                 vis_ref, stats, toks, data):
    cbs = x_ref.shape[0]
    slots = peers * cap
    stats[...] = stats_columns(sums_ref, width)
    data[...] = jnp.zeros_like(data)
    for cb in range(cbs):
        ch = slice(cb * LANES, (cb + 1) * LANES)

        def body(b, c, cb=cb, ch=ch):
            here = pl.ds(pl.multiple_of(b * 8, 8), 8)
            st = stats[here, :]
            for p in range(POS):
                n = (f_ref[cb, p, here, :] - st[:, p : p + 1]) * st[:, POS + p : POS + p + 1]
                m = n * gain_ref[:, ch] + shift_ref[:, ch]
                toks[cb, pl.ds(b * 8 * POS + p, 8, stride=POS), :] = x_ref[cb, p, here, :] + scale_ref[:, ch] * m
            return c

        lax.fori_loop(0, slots // 8, body, 0)

    def put(s, c):
        at = pl.ds(pl.multiple_of(off_ref[s] * POS, POS), POS)
        for cb in range(cbs):
            data[cb, at, :] = toks[cb, pl.ds(pl.multiple_of(s * POS, POS), POS), :]
        return c

    lax.fori_loop(0, slots, put, 0, unroll=8)
    for cb in range(cbs):
        vis_ref[:, cb * LANES : (cb + 1) * LANES] = data[cb, 0 : vis_ref.shape[0], :].astype(jnp.bfloat16)


def unpack_kernel(cap, slot_ref, back_ref, out_ref, data, rows):
    tiles = slot_ref.shape[0]
    cbs = out_ref.shape[1] // LANES
    part = cbs * cap * POS
    data[...] = back_ref[...].astype(jnp.float32)

    def move(t, c):
        slot = slot_ref[t]
        d, r = slot // cap, lax.rem(slot, cap)
        for cb in range(cbs):
            at = pl.multiple_of(d * part + cb * cap * POS + r * POS, POS)
            rows[cb, pl.ds(pl.multiple_of(t * POS, POS), POS), :] = data[pl.ds(at, POS), :]
        return c

    lax.fori_loop(0, tiles, move, 0, unroll=8)
    for cb in range(cbs):
        out_ref[:, cb * LANES : (cb + 1) * LANES] = rows[cb].astype(jnp.bfloat16)


def finish_kernel(parts_ref, gain_ref, shift_ref, scale_ref, out_ref):
    total = parts_ref[0]
    for i in range(1, parts_ref.shape[0]):
        total = total + parts_ref[i]
    out_ref[...] = jnp.zeros_like(out_ref)
    n, taps = len(USED), out_ref.shape[0] - 4
    for i, tap in enumerate(USED):
        out_ref[tap : tap + 1, :] = total[i : i + 1]
    along, plain = total[n + 1 : n + 2], total[n + 2 : n + 3]
    out_ref[taps : taps + 1, :] = total[n : n + 1]
    out_ref[taps + 1 : taps + 2, :] = along * scale_ref[...]
    out_ref[taps + 2 : taps + 3, :] = plain * scale_ref[...]
    out_ref[taps + 3 : taps + 4, :] = along * gain_ref[...] + plain * shift_ref[...]


ANY = pl.BlockSpec(memory_space=pl.ANY)
SMEM = pl.BlockSpec(memory_space=pltpu.SMEM)
VMEM = pl.BlockSpec(memory_space=pltpu.VMEM)


def call(kernel, ins, outs, scratch, out_specs):
    return pl.pallas_call(
        kernel,
        out_shape=outs,
        in_specs=ins,
        out_specs=out_specs,
        scratch_shapes=scratch,
        compiler_params=pltpu.CompilerParams(vmem_limit_bytes=VMEM_LIMIT),
    )


def per_device(tile_features, dw_kernel, dw_bias, ln_gain, ln_shift, layer_scale,
               sample_counts, tile_dest, tile_offset, seq_grad):
    tiles_dev, _, _, chans = tile_features.shape
    enc = lax.axis_size(ENC)
    width = float(chans * enc)
    peers = lax.axis_size(DP)
    cap = tiles_dev // peers + 1
    slots, cbs = peers * cap, chans // LANES
    blocks = seq_grad.shape[0] // POS
    part_out = cbs * cap * POS
    part = part_out + 2
    f32, i32, bf16 = jnp.float32, jnp.int32, jnp.bfloat16
    shape = jax.ShapeDtypeStruct
    bias, gain, shift, scale = (v.reshape(1, chans) for v in (dw_bias, ln_gain, ln_shift, layer_scale))
    grid = shape((cbs, POS, slots, LANES), f32)

    ints = jnp.concatenate([tile_dest, tile_offset, sample_counts], 1)
    send, slot = call(
        functools.partial(pack_kernel, peers, cap, part),
        [ANY, VMEM],
        (shape((peers * part, LANES), bf16), shape((tiles_dev,), i32)),
        [pltpu.VMEM((cbs, tiles_dev * POS, LANES), f32), pltpu.VMEM((peers * part, LANES), f32), pltpu.SMEM((peers,), i32),
         pltpu.SMEM(ints.shape, i32), pltpu.SemaphoreType.DMA],
        (VMEM, SMEM),
    )(ints, tile_features.reshape(tiles_dev * POS, chans))
    got = lax.all_to_all(send.reshape(peers, part // 2, 2, LANES), DP, split_axis=0, concat_axis=0, tiled=True)
    x, u, f, sums, off = call(
        functools.partial(conv_kernel, peers, cap, part),
        [VMEM] * 6,
        (grid, grid, grid, shape((enc, 4 * POS, slots), f32), shape((slots,), i32)),
        [
            pltpu.VMEM((peers * part, LANES), f32),
            pltpu.VMEM((cbs, (blocks + 1) * POS, LANES), f32),
            pltpu.VMEM((cbs, slots * POS, LANES), f32),
            pltpu.VMEM((slots, LANES), f32),
            pltpu.VMEM((8, LANES), i32),
            pltpu.VMEM((8, LANES), f32),
            pltpu.SMEM((8, LANES), i32),
            pltpu.SMEM((8, LANES), f32),
            pltpu.SemaphoreType.DMA((2,)),
        ],
        (VMEM, VMEM, VMEM, VMEM, SMEM),
    )(got.reshape(peers * part, LANES), seq_grad, dw_kernel, bias, gain, scale)
    sums = lax.all_to_all(sums, ENC, split_axis=0, concat_axis=0, tiled=True)
    outgoing, grads = call(
        functools.partial(grad_kernel, peers, cap, width),
        [VMEM] * 7,
        (shape((peers * part_out, LANES), bf16), shape((ROWS, chans), f32)),
        [pltpu.VMEM((slots, LANES), f32), pltpu.VMEM((peers * part_out, LANES), f32), pltpu.VMEM((ROWS, 8, chans), f32)],
        (VMEM, VMEM),
    )(sums, x, u, f, dw_kernel, gain, scale)
    back = lax.all_to_all(outgoing.reshape(peers, part_out, LANES), DP, split_axis=0, concat_axis=0, tiled=True)
    grads = lax.psum(lax.psum(grads, "y"), "zh")
    inner = lax.axis_size("zl")
    grads, back, off, sums = lax.optimization_barrier((grads, back, off, sums))
    parts = lax.all_to_all(
        jnp.broadcast_to(grads, (inner, ROWS, chans)), "zl", split_axis=0, concat_axis=0, tiled=True
    )
    tile_grads = call(
        functools.partial(unpack_kernel, cap),
        [SMEM, VMEM],
        shape((tiles_dev * POS, chans), bf16),
        [pltpu.VMEM((peers * part_out, LANES), f32), pltpu.VMEM((cbs, tiles_dev * POS, LANES), f32)],
        VMEM,
    )(slot, back.reshape(peers * part_out, LANES))
    vis = call(
        functools.partial(token_kernel, peers, cap, width),
        [SMEM] + [VMEM] * 6,
        shape((blocks * POS, chans), bf16),
        [
            pltpu.VMEM((slots, LANES), f32),
            pltpu.VMEM((cbs, slots * POS, LANES), f32),
            pltpu.VMEM((cbs, (blocks + 1) * POS, LANES), f32),
        ],
        VMEM,
    )(off, sums, x, f, gain, shift, scale)
    param_grads = call(
        finish_kernel, [VMEM] * 4, shape((dw_kernel.shape[0] + 4, chans), f32), [], VMEM
    )(parts, gain, shift, scale)
    return vis, tile_grads.reshape(tile_features.shape), param_grads


def solution(mesh):
    grid = Mesh(mesh.devices.reshape(4, 4, 4, 4, 2), DP + ENC)
    placed = (
        P(DP, None, None, ENC),
        P(None, ENC),
        P(ENC),
        P(ENC),
        P(ENC),
        P(ENC),
        P(DP, None),
        P(DP, None),
        P(DP, None),
        P(DP, ENC),
    )
    return jax.shard_map(
        per_device,
        mesh=grid,
        in_specs=placed,
        out_specs=(P(DP, ENC), P(DP, None, None, ENC), P(None, ENC)),
        check_vma=False,
    )
```

```python
import functools

import jax
import jax.numpy as jnp
from jax import lax
from jax.experimental import pallas as pl
from jax.experimental.pallas import tpu as pltpu
from jax.sharding import Mesh
from jax.sharding import PartitionSpec as P

EPS = 1e-06
HGT, WID = 4, 2
POS = HGT * WID
LANES = 128
DP = ("zh", "zl", "y")
ENC = ("x", "core")
VMEM_LIMIT = 16 * 1024 * 1024


def full(a, b):
    (ha, wa), (hb, wb) = divmod(a, WID), divmod(b, WID)
    return (hb - ha + 3) * 7 + (wb - wa + 3)


USED = sorted({full(a, b) for a in range(POS) for b in range(POS)})
PLACE = {tap: i for i, tap in enumerate(USED)}
ROWS = len(USED) + 3


def pack_kernel(peers, cap, part, ints_hbm, tiles_ref, send_ref, slot_ref, rows, data, seen, ints, sem):
    fetch = pltpu.make_async_copy(ints_hbm, ints, sem)
    fetch.start()
    tiles = tiles_ref.shape[0] // POS
    cbs = tiles_ref.shape[1] // LANES
    meta = cbs * cap * POS
    data[...] = jnp.zeros_like(data)
    for cb in range(cbs):
        rows[cb] = tiles_ref[:, cb * LANES : (cb + 1) * LANES].astype(jnp.float32)

    def clear(i, c):
        seen[i] = 0
        return c

    lax.fori_loop(0, peers, clear, 0, unroll=8)
    fetch.wait()
    lane = lax.broadcasted_iota(jnp.int32, (1, LANES), 1)

    def move(t, carry):
        s, end = carry
        step = (t >= end).astype(jnp.int32)
        s = s + step
        count = ints[0, 2 * tiles + s]
        end = end + step * count
        d = ints[0, t]
        r = seen[d]
        seen[d] = r + 1
        slot_ref[t] = d * cap + r
        for cb in range(cbs):
            at = d * part + cb * cap * POS + r * POS
            data[pl.ds(at, POS), :] = rows[cb, pl.ds(pl.multiple_of(t * POS, POS), POS), :]
        note = jnp.where(lane == r, ints[0, tiles + t], jnp.where(lane == cap + r, count, 0))
        here = pl.ds(d * part + meta, 1)
        data[here, :] = data[here, :] + note.astype(jnp.float32)
        return s, end

    lax.fori_loop(0, tiles, move, (jnp.int32(0), ints[0, 2 * tiles]), unroll=4)
    send_ref[...] = data[...].astype(jnp.bfloat16)


def conv_kernel(peers, cap, part, got_ref, seq_ref, kern_ref, bias_ref, gain_ref, scale_ref,
                data, ups, f_ref, sums_ref, off_ref, seq, cols, off_v, wgt_v, off_s, wgt_s, sem):
    cbs = seq.shape[0]
    blocks = seq.shape[1] // POS - 1
    meta = cbs * cap * POS
    data[...] = got_ref[...].astype(jnp.float32)
    notes = data[pl.ds(meta, peers, stride=part), :]
    notes = jnp.concatenate([notes, jnp.zeros((LANES - peers, LANES), jnp.float32)], 0).T
    count = notes[cap : 2 * cap]
    off_v[0:cap] = jnp.where(count > 0.5, notes[0:cap], float(blocks)).astype(jnp.int32)
    wgt_v[0:cap] = jnp.where(count > 0.5, 8.0 / jnp.maximum(count, 1.0), 0.0)
    moves = [pltpu.make_async_copy(off_v, off_s, sem.at[0]), pltpu.make_async_copy(wgt_v, wgt_s, sem.at[1])]
    for m in moves:
        m.start()
    for cb in range(cbs):
        seq[cb, 0 : blocks * POS, :] = seq_ref[:, cb * LANES : (cb + 1) * LANES].astype(jnp.float32)
        seq[cb, blocks * POS :, :] = jnp.zeros((POS, LANES), jnp.float32)
    for m in moves:
        m.wait()
    for r in range(cap):

        def fetch(d, c, r=r):
            off, w = off_s[r, d], wgt_s[r, d]
            off_ref[r * peers + d] = off
            for cb in range(cbs):
                ups[cb, pl.ds(pl.multiple_of((r * peers + d) * POS, POS), POS), :] = (
                    seq[cb, pl.ds(pl.multiple_of(off * POS, POS), POS), :] * w
                )
            return c

        lax.fori_loop(0, peers, fetch, 0, unroll=8)
    lane = lax.broadcasted_iota(jnp.int32, (8, LANES), 1)
    for r in range(cap):

        def body(b, c, r=r):
            here = pl.ds(pl.multiple_of(r * peers + b * 8, 8), 8)
            xs = {}
            for cb in range(cbs):
                for q in range(POS):
                    xs[cb, q] = data[pl.ds(b * 8 * part + cb * cap * POS + r * POS + q, 8, stride=part), :]
            out = jnp.zeros((8, LANES), jnp.float32)
            for p in range(POS):
                tot = [None] * 4
                for cb in range(cbs):
                    ch = slice(cb * LANES, (cb + 1) * LANES)
                    f = bias_ref[:, ch] + kern_ref[full(p, 0) : full(p, 0) + 1, ch] * xs[cb, 0]
                    for q in range(1, POS):
                        f = f + kern_ref[full(p, q) : full(p, q) + 1, ch] * xs[cb, q]
                    f_ref[cb, p, here, :] = f
                    u = ups[cb, pl.ds((r * peers + b * 8) * POS + p, 8, stride=POS), :]
                    dn = u * (scale_ref[:, ch] * gain_ref[:, ch])
                    new = [f, f * f, dn, dn * f]
                    tot = new if cb == 0 else [a + n for a, n in zip(tot, new)]
                for k in range(4):
                    out = jnp.where(lane == k * POS + p, jnp.sum(tot[k], 1, keepdims=True), out)
            cols[here, :] = out
            return c

        lax.fori_loop(0, peers // 8, body, 0)
    total = cols[...].T[0 : 4 * POS]
    for i in range(sums_ref.shape[0]):
        sums_ref[i] = total


def stats_columns(sums_ref, width):
    sums = sums_ref[0]
    for i in range(1, sums_ref.shape[0]):
        sums = sums + sums_ref[i]
    center = sums[0:POS] / width
    inv = lax.rsqrt(jnp.maximum(sums[POS : 2 * POS] / width - center * center, 0.0) + EPS)
    first = sums[2 * POS : 3 * POS]
    second = inv * (sums[3 * POS : 4 * POS] - center * first)
    slots = sums.shape[1]
    rows = [center, inv, first / width, second / width, jnp.zeros((LANES - 4 * POS, slots), jnp.float32)]
    return jnp.concatenate(rows, 0).T


def grad_kernel(peers, cap, part, extra, width, sums_ref, data_ref, ups_ref, f_ref, kern_ref, gain_ref, scale_ref,
                out_ref, stats, data, acc, even, odd):
    cbs = f_ref.shape[0]
    meta = cbs * cap * POS
    back = meta + extra
    stats[...] = stats_columns(sums_ref, width)
    acc[...] = jnp.zeros_like(acc)
    for r in range(cap):

        def body(b, c, r=r):
            here = pl.ds(pl.multiple_of(r * peers + b * 8, 8), 8)
            st = stats[here, :]
            for cb in range(cbs):
                ch = slice(cb * LANES, (cb + 1) * LANES)

                def add(row, v):
                    acc[row, :, ch] = acc[row, :, ch] + v

                df, xs, us = [], [], []
                a_sum = b_sum = d_sum = None
                for p in range(POS):
                    col = [st[:, k * POS + p : k * POS + p + 1] for k in range(4)]
                    u = ups_ref[cb, pl.ds((r * peers + b * 8) * POS + p, 8, stride=POS), :]
                    n = (f_ref[cb, p, here, :] - col[0]) * col[1]
                    d = col[1] * (u * (scale_ref[:, ch] * gain_ref[:, ch]) - col[2] - n * col[3])
                    df.append(d)
                    us.append(u)
                    xs.append(data_ref[pl.ds(b * 8 * part + cb * cap * POS + r * POS + p, 8, stride=part), :])
                    a_sum = u * n if p == 0 else a_sum + u * n
                    b_sum = u if p == 0 else b_sum + u
                    d_sum = d if p == 0 else d_sum + d
                taps = {}
                for p in range(POS):
                    for q in range(POS):
                        t = PLACE[full(p, q)]
                        v = df[p] * xs[q]
                        taps[t] = v if t not in taps else taps[t] + v
                for t, v in taps.items():
                    add(t, v)
                add(len(USED), d_sum)
                add(len(USED) + 1, a_sum)
                add(len(USED) + 2, b_sum)
                for q in range(POS):
                    t = us[q]
                    for p in range(POS):
                        t = t + kern_ref[full(p, q) : full(p, q) + 1, ch] * df[p]
                    data[pl.ds(b * 8 * back + cb * cap * POS + r * POS + q, 8, stride=back), :] = t
            return c

        lax.fori_loop(0, peers // 8, body, 0)
    for row in range(ROWS):
        for cb in range(cbs):
            v = row * cbs + cb
            half = even if v % 2 == 0 else odd
            half[v // 2 : v // 2 + 1, :] = jnp.sum(acc[row, :, cb * LANES : (cb + 1) * LANES], 0, keepdims=True)
    holders = even.shape[0]
    for i, half in enumerate((even, odd)):
        sums = half[...]
        high = sums.astype(jnp.bfloat16).astype(jnp.float32)
        for j, v in ((i, high), (i + 2, sums - high)):
            data[pl.ds(meta + j, holders, stride=back), :] = v
    for j in range(extra):
        data[pl.ds(holders * back + meta + j, peers - holders, stride=back), :] = jnp.zeros((peers - holders, LANES), jnp.float32)
    out_ref[...] = data[...].astype(jnp.bfloat16)


def token_kernel(peers, cap, part, width, off_ref, sums_ref, data_ref, f_ref, gain_ref, shift_ref, scale_ref,
                 vis_ref, stats, toks, data):
    cbs = f_ref.shape[0]
    slots = peers * cap
    stats[...] = stats_columns(sums_ref, width)
    data[...] = jnp.zeros_like(data)
    for r in range(cap):

        def body(b, c, r=r):
            here = pl.ds(pl.multiple_of(r * peers + b * 8, 8), 8)
            st = stats[here, :]
            for cb in range(cbs):
                ch = slice(cb * LANES, (cb + 1) * LANES)
                for p in range(POS):
                    n = (f_ref[cb, p, here, :] - st[:, p : p + 1]) * st[:, POS + p : POS + p + 1]
                    m = n * gain_ref[:, ch] + shift_ref[:, ch]
                    x = data_ref[pl.ds(b * 8 * part + cb * cap * POS + r * POS + p, 8, stride=part), :]
                    toks[cb, pl.ds((r * peers + b * 8) * POS + p, 8, stride=POS), :] = x + scale_ref[:, ch] * m
            return c

        lax.fori_loop(0, peers // 8, body, 0)

    def put(s, c):
        at = pl.ds(pl.multiple_of(off_ref[s] * POS, POS), POS)
        for cb in range(cbs):
            data[cb, at, :] = toks[cb, pl.ds(pl.multiple_of(s * POS, POS), POS), :]
        return c

    lax.fori_loop(0, slots, put, 0, unroll=8)
    for cb in range(cbs):
        vis_ref[:, cb * LANES : (cb + 1) * LANES] = data[cb, 0 : vis_ref.shape[0], :].astype(jnp.bfloat16)


def total_kernel(meta, back, back_ref, out_ref):
    peers = out_ref.shape[0]
    rows = back_ref.shape[0]
    at = lax.rem(lax.broadcasted_iota(jnp.int32, (8, rows), 1), back) - meta
    which = lax.broadcasted_iota(jnp.int32, (8, rows), 0)
    pick = jnp.where((at == which) | (at == which + 2), 1.0, 0.0)
    pick = jnp.where(which < 2, pick, 0.0).astype(jnp.bfloat16)
    total = jnp.dot(pick, back_ref[...], preferred_element_type=jnp.float32)[0:2]
    out_ref[...] = jnp.broadcast_to(total[None], (peers, 2, LANES))


def unpack_kernel(cap, part, slot_ref, back_ref, out_ref, data, rows):
    tiles = slot_ref.shape[0]
    cbs = out_ref.shape[1] // LANES
    data[...] = back_ref[...].astype(jnp.float32)

    def move(t, c):
        slot = slot_ref[t]
        d, r = slot // cap, lax.rem(slot, cap)
        for cb in range(cbs):
            at = d * part + cb * cap * POS + r * POS
            rows[cb, pl.ds(pl.multiple_of(t * POS, POS), POS), :] = data[pl.ds(at, POS), :]
        return c

    lax.fori_loop(0, tiles, move, 0, unroll=8)
    for cb in range(cbs):
        out_ref[:, cb * LANES : (cb + 1) * LANES] = rows[cb].astype(jnp.bfloat16)


def finish_kernel(parts_ref, gain_ref, shift_ref, scale_ref, out_ref):
    out_ref[...] = jnp.zeros_like(out_ref)
    n, taps = len(USED), out_ref.shape[0] - 4
    cbs = out_ref.shape[1] // LANES
    for cb in range(cbs):
        ch = slice(cb * LANES, (cb + 1) * LANES)

        def total(i):
            v = i * cbs + cb
            return parts_ref[v // 2, v % 2 : v % 2 + 1, :]

        for i, tap in enumerate(USED):
            out_ref[tap : tap + 1, ch] = total(i)
        along, plain = total(n + 1), total(n + 2)
        out_ref[taps : taps + 1, ch] = total(n)
        out_ref[taps + 1 : taps + 2, ch] = along * scale_ref[:, ch]
        out_ref[taps + 2 : taps + 3, ch] = plain * scale_ref[:, ch]
        out_ref[taps + 3 : taps + 4, ch] = along * gain_ref[:, ch] + plain * shift_ref[:, ch]


ANY = pl.BlockSpec(memory_space=pl.ANY)
SMEM = pl.BlockSpec(memory_space=pltpu.SMEM)
VMEM = pl.BlockSpec(memory_space=pltpu.VMEM)


def call(kernel, ins, outs, scratch, out_specs):
    return pl.pallas_call(
        kernel,
        out_shape=outs,
        in_specs=ins,
        out_specs=out_specs,
        scratch_shapes=scratch,
        compiler_params=pltpu.CompilerParams(vmem_limit_bytes=VMEM_LIMIT),
    )


def per_device(tile_features, dw_kernel, dw_bias, ln_gain, ln_shift, layer_scale,
               sample_counts, tile_dest, tile_offset, seq_grad):
    tiles_dev, _, _, chans = tile_features.shape
    enc = lax.axis_size(ENC)
    width = float(chans * enc)
    peers = lax.axis_size(DP)
    cap = tiles_dev // peers + 1
    slots, cbs = peers * cap, chans // LANES
    blocks = seq_grad.shape[0] // POS
    meta, extra = cbs * cap * POS, 4
    part, back_part = meta + 2, meta + extra
    holders = ROWS * cbs // 2
    f32, i32, bf16 = jnp.float32, jnp.int32, jnp.bfloat16
    shape = jax.ShapeDtypeStruct
    bias, gain, shift, scale = (v.reshape(1, chans) for v in (dw_bias, ln_gain, ln_shift, layer_scale))

    def swap(v, axes):
        return lax.all_to_all(v, axes, split_axis=0, concat_axis=0, tiled=True)


    ints = jnp.concatenate([tile_dest, tile_offset, sample_counts], 1)
    send, slot = call(
        functools.partial(pack_kernel, peers, cap, part),
        [ANY, VMEM],
        (shape((peers * part, LANES), bf16), shape((tiles_dev,), i32)),
        [pltpu.VMEM((cbs, tiles_dev * POS, LANES), f32), pltpu.VMEM((peers * part, LANES), f32), pltpu.SMEM((peers,), i32),
         pltpu.SMEM(ints.shape, i32), pltpu.SemaphoreType.DMA],
        (VMEM, SMEM),
    )(ints, tile_features.reshape(tiles_dev * POS, chans))
    got = swap(send.reshape(peers, part // 2, 2, LANES), DP)
    data, ups, f, sums, off = call(
        functools.partial(conv_kernel, peers, cap, part),
        [VMEM] * 6,
        (
            shape((peers * part, LANES), f32),
            shape((cbs, slots * POS, LANES), f32),
            shape((cbs, POS, slots, LANES), f32),
            shape((enc, 4 * POS, slots), f32),
            shape((slots,), i32),
        ),
        [
            pltpu.VMEM((cbs, (blocks + 1) * POS, LANES), f32),
            pltpu.VMEM((slots, LANES), f32),
            pltpu.VMEM((8, LANES), i32),
            pltpu.VMEM((8, LANES), f32),
            pltpu.SMEM((8, LANES), i32),
            pltpu.SMEM((8, LANES), f32),
            pltpu.SemaphoreType.DMA((2,)),
        ],
        (VMEM, VMEM, VMEM, VMEM, SMEM),
    )(got.reshape(peers * part, LANES), seq_grad, dw_kernel, bias, gain, scale)
    sums = swap(sums, ENC)
    outgoing = call(
        functools.partial(grad_kernel, peers, cap, part, extra, width),
        [VMEM] * 7,
        shape((peers * back_part, LANES), bf16),
        [
            pltpu.VMEM((slots, LANES), f32),
            pltpu.VMEM((peers * back_part, LANES), f32),
            pltpu.VMEM((ROWS, 8, chans), f32),
            pltpu.VMEM((holders, LANES), f32),
            pltpu.VMEM((holders, LANES), f32),
        ],
        VMEM,
    )(sums, data, ups, f, dw_kernel, gain, scale)
    back = swap(outgoing.reshape(peers, back_part // 2, 2, LANES), DP).reshape(peers * back_part, LANES)
    vis = call(
        functools.partial(token_kernel, peers, cap, part, width),
        [SMEM] + [VMEM] * 6,
        shape((blocks * POS, chans), bf16),
        [
            pltpu.VMEM((slots, LANES), f32),
            pltpu.VMEM((cbs, slots * POS, LANES), f32),
            pltpu.VMEM((cbs, (blocks + 1) * POS, LANES), f32),
        ],
        VMEM,
    )(off, sums, data, f, gain, shift, scale)
    mine = call(functools.partial(total_kernel, meta, back_part), [VMEM], shape((peers, 2, LANES), f32), [], VMEM)(back)
    parts = swap(mine, DP)
    tile_grads = call(
        functools.partial(unpack_kernel, cap, back_part),
        [SMEM, VMEM],
        shape((tiles_dev * POS, chans), bf16),
        [pltpu.VMEM((peers * back_part, LANES), f32), pltpu.VMEM((cbs, tiles_dev * POS, LANES), f32)],
        VMEM,
    )(slot, back)
    param_grads = call(
        finish_kernel, [VMEM] * 4, shape((dw_kernel.shape[0] + 4, chans), f32), [], VMEM
    )(parts, gain, shift, scale)
    return vis, tile_grads.reshape(tile_features.shape), param_grads


def solution(mesh):
    grid = Mesh(mesh.devices.reshape(4, 4, 4, 4, 2), DP + ENC)
    placed = (
        P(DP, None, None, ENC),
        P(None, ENC),
        P(ENC),
        P(ENC),
        P(ENC),
        P(ENC),
        P(DP, None),
        P(DP, None),
        P(DP, None),
        P(DP, ENC),
    )
    return jax.shard_map(
        per_device,
        mesh=grid,
        in_specs=placed,
        out_specs=(P(DP, ENC), P(DP, None, None, ENC), P(None, ENC)),
        check_vma=False,
    )
```

```python
import functools

import jax
import jax.numpy as jnp
from jax import lax
from jax.experimental import pallas as pl
from jax.experimental.pallas import tpu as pltpu
from jax.sharding import Mesh
from jax.sharding import PartitionSpec as P

EPS = 1e-06
HGT, WID = 4, 2
POS = HGT * WID
LANES = 128
DP = ("zh", "zl", "y")
NEAR = ("zl", "y")
ENC = ("x", "core")
VMEM_LIMIT = 16 * 1024 * 1024


def full(a, b):
    (ha, wa), (hb, wb) = divmod(a, WID), divmod(b, WID)
    return (hb - ha + 3) * 7 + (wb - wa + 3)


USED = sorted({full(a, b) for a in range(POS) for b in range(POS)})
PLACE = {tap: i for i, tap in enumerate(USED)}
ROWS = len(USED) + 3


def pack_kernel(peers, cap, part, ints_hbm, tiles_ref, send_ref, slot_ref, rows, data, seen, ints, sem):
    fetch = pltpu.make_async_copy(ints_hbm, ints, sem)
    fetch.start()
    tiles = tiles_ref.shape[0] // POS
    cbs = tiles_ref.shape[1] // LANES
    meta = cbs * cap * POS
    data[...] = jnp.zeros_like(data)
    for cb in range(cbs):
        rows[cb] = tiles_ref[:, cb * LANES : (cb + 1) * LANES].astype(jnp.float32)

    def clear(i, c):
        seen[i] = 0
        return c

    lax.fori_loop(0, peers, clear, 0, unroll=8)
    fetch.wait()
    lane = lax.broadcasted_iota(jnp.int32, (1, LANES), 1)

    def move(t, carry):
        s, end = carry
        step = (t >= end).astype(jnp.int32)
        s = s + step
        count = ints[0, 2 * tiles + s]
        end = end + step * count
        d = ints[0, t]
        r = seen[d]
        seen[d] = r + 1
        slot_ref[t] = d * cap + r
        for cb in range(cbs):
            at = d * part + cb * cap * POS + r * POS
            data[pl.ds(at, POS), :] = rows[cb, pl.ds(pl.multiple_of(t * POS, POS), POS), :]
        note = jnp.where(lane == r, ints[0, tiles + t], jnp.where(lane == cap + r, count, 0))
        here = pl.ds(d * part + meta, 1)
        data[here, :] = data[here, :] + note.astype(jnp.float32)
        return s, end

    lax.fori_loop(0, tiles, move, (jnp.int32(0), ints[0, 2 * tiles]), unroll=4)
    send_ref[...] = data[...].astype(jnp.bfloat16)


def conv_kernel(peers, cap, part, got_ref, seq_ref, kern_ref, bias_ref, gain_ref, scale_ref,
                data, ups, f_ref, sums_ref, off_ref, seq, cols, off_v, wgt_v, off_s, wgt_s, sem):
    cbs = seq.shape[0]
    blocks = seq.shape[1] // POS - 1
    meta = cbs * cap * POS
    data[...] = got_ref[...].astype(jnp.float32)
    notes = data[pl.ds(meta, peers, stride=part), :]
    notes = jnp.concatenate([notes, jnp.zeros((LANES - peers, LANES), jnp.float32)], 0).T
    count = notes[cap : 2 * cap]
    off_v[0:cap] = jnp.where(count > 0.5, notes[0:cap], float(blocks)).astype(jnp.int32)
    wgt_v[0:cap] = jnp.where(count > 0.5, 8.0 / jnp.maximum(count, 1.0), 0.0)
    moves = [pltpu.make_async_copy(off_v, off_s, sem.at[0]), pltpu.make_async_copy(wgt_v, wgt_s, sem.at[1])]
    for m in moves:
        m.start()
    for cb in range(cbs):
        seq[cb, 0 : blocks * POS, :] = seq_ref[:, cb * LANES : (cb + 1) * LANES].astype(jnp.float32)
        seq[cb, blocks * POS :, :] = jnp.zeros((POS, LANES), jnp.float32)
    for m in moves:
        m.wait()
    for r in range(cap):

        def fetch(d, c, r=r):
            off, w = off_s[r, d], wgt_s[r, d]
            off_ref[r * peers + d] = off
            for cb in range(cbs):
                ups[cb, pl.ds(pl.multiple_of((r * peers + d) * POS, POS), POS), :] = (
                    seq[cb, pl.ds(pl.multiple_of(off * POS, POS), POS), :] * w
                )
            return c

        lax.fori_loop(0, peers, fetch, 0, unroll=8)
    lane = lax.broadcasted_iota(jnp.int32, (8, LANES), 1)
    for r in range(cap):

        def body(b, c, r=r):
            here = pl.ds(pl.multiple_of(r * peers + b * 8, 8), 8)
            xs = {}
            for cb in range(cbs):
                for q in range(POS):
                    xs[cb, q] = data[pl.ds(b * 8 * part + cb * cap * POS + r * POS + q, 8, stride=part), :]
            out = jnp.zeros((8, LANES), jnp.float32)
            for p in range(POS):
                tot = [None] * 4
                for cb in range(cbs):
                    ch = slice(cb * LANES, (cb + 1) * LANES)
                    f = bias_ref[:, ch] + kern_ref[full(p, 0) : full(p, 0) + 1, ch] * xs[cb, 0]
                    for q in range(1, POS):
                        f = f + kern_ref[full(p, q) : full(p, q) + 1, ch] * xs[cb, q]
                    f_ref[cb, p, here, :] = f
                    u = ups[cb, pl.ds((r * peers + b * 8) * POS + p, 8, stride=POS), :]
                    dn = u * (scale_ref[:, ch] * gain_ref[:, ch])
                    new = [f, f * f, dn, dn * f]
                    tot = new if cb == 0 else [a + n for a, n in zip(tot, new)]
                for k in range(4):
                    out = jnp.where(lane == k * POS + p, jnp.sum(tot[k], 1, keepdims=True), out)
            cols[here, :] = out
            return c

        lax.fori_loop(0, peers // 8, body, 0)
    total = cols[...].T[0 : 4 * POS]
    for i in range(sums_ref.shape[0]):
        sums_ref[i] = total


def stats_columns(sums_ref, width):
    sums = sums_ref[0]
    for i in range(1, sums_ref.shape[0]):
        sums = sums + sums_ref[i]
    center = sums[0:POS] / width
    inv = lax.rsqrt(jnp.maximum(sums[POS : 2 * POS] / width - center * center, 0.0) + EPS)
    first = sums[2 * POS : 3 * POS]
    second = inv * (sums[3 * POS : 4 * POS] - center * first)
    slots = sums.shape[1]
    rows = [center, inv, first / width, second / width, jnp.zeros((LANES - 4 * POS, slots), jnp.float32)]
    return jnp.concatenate(rows, 0).T


def grad_kernel(peers, near, cap, part, each, width, sums_ref, data_ref, ups_ref, f_ref, kern_ref, gain_ref, scale_ref,
                out_ref, stats, data, acc, partial):
    cbs = f_ref.shape[0]
    meta = cbs * cap * POS
    back = meta + 2 * each
    stats[...] = stats_columns(sums_ref, width)
    acc[...] = jnp.zeros_like(acc)
    for r in range(cap):

        def body(b, c, r=r):
            here = pl.ds(pl.multiple_of(r * peers + b * 8, 8), 8)
            st = stats[here, :]
            for cb in range(cbs):
                ch = slice(cb * LANES, (cb + 1) * LANES)

                def add(row, v):
                    acc[row, :, ch] = acc[row, :, ch] + v

                df, xs, us = [], [], []
                a_sum = b_sum = d_sum = None
                for p in range(POS):
                    col = [st[:, k * POS + p : k * POS + p + 1] for k in range(4)]
                    u = ups_ref[cb, pl.ds((r * peers + b * 8) * POS + p, 8, stride=POS), :]
                    n = (f_ref[cb, p, here, :] - col[0]) * col[1]
                    d = col[1] * (u * (scale_ref[:, ch] * gain_ref[:, ch]) - col[2] - n * col[3])
                    df.append(d)
                    us.append(u)
                    xs.append(data_ref[pl.ds(b * 8 * part + cb * cap * POS + r * POS + p, 8, stride=part), :])
                    a_sum = u * n if p == 0 else a_sum + u * n
                    b_sum = u if p == 0 else b_sum + u
                    d_sum = d if p == 0 else d_sum + d
                taps = {}
                for p in range(POS):
                    for q in range(POS):
                        t = PLACE[full(p, q)]
                        v = df[p] * xs[q]
                        taps[t] = v if t not in taps else taps[t] + v
                for t, v in taps.items():
                    add(t, v)
                add(len(USED), d_sum)
                add(len(USED) + 1, a_sum)
                add(len(USED) + 2, b_sum)
                for q in range(POS):
                    t = us[q]
                    for p in range(POS):
                        t = t + kern_ref[full(p, q) : full(p, q) + 1, ch] * df[p]
                    data[pl.ds(b * 8 * back + cb * cap * POS + r * POS + q, 8, stride=back), :] = t
            return c

        lax.fori_loop(0, peers // 8, body, 0)
    for row in range(ROWS):
        for cb in range(cbs):
            v = row * cbs + cb
            partial[v : v + 1, :] = jnp.sum(acc[row, :, cb * LANES : (cb + 1) * LANES], 0, keepdims=True)
    partial[ROWS * cbs :, :] = jnp.zeros((each * near - ROWS * cbs, LANES), jnp.float32)
    for i in range(each):
        sums = partial[pl.ds(i, near, stride=each), :]
        high = sums.astype(jnp.bfloat16).astype(jnp.float32)
        for j, v in ((i, high), (i + each, sums - high)):
            for far in range(peers // near):
                data[pl.ds(far * near * back + meta + j, near, stride=back), :] = v
    out_ref[...] = data[...].astype(jnp.bfloat16)


def token_kernel(peers, cap, part, width, off_ref, sums_ref, data_ref, f_ref, gain_ref, shift_ref, scale_ref,
                 vis_ref, stats, toks, data):
    cbs = f_ref.shape[0]
    slots = peers * cap
    stats[...] = stats_columns(sums_ref, width)
    data[...] = jnp.zeros_like(data)
    for r in range(cap):

        def body(b, c, r=r):
            here = pl.ds(pl.multiple_of(r * peers + b * 8, 8), 8)
            st = stats[here, :]
            for cb in range(cbs):
                ch = slice(cb * LANES, (cb + 1) * LANES)
                for p in range(POS):
                    n = (f_ref[cb, p, here, :] - st[:, p : p + 1]) * st[:, POS + p : POS + p + 1]
                    m = n * gain_ref[:, ch] + shift_ref[:, ch]
                    x = data_ref[pl.ds(b * 8 * part + cb * cap * POS + r * POS + p, 8, stride=part), :]
                    toks[cb, pl.ds((r * peers + b * 8) * POS + p, 8, stride=POS), :] = x + scale_ref[:, ch] * m
            return c

        lax.fori_loop(0, peers // 8, body, 0)

    def put(s, c):
        at = pl.ds(pl.multiple_of(off_ref[s] * POS, POS), POS)
        for cb in range(cbs):
            data[cb, at, :] = toks[cb, pl.ds(pl.multiple_of(s * POS, POS), POS), :]
        return c

    lax.fori_loop(0, slots, put, 0, unroll=8)
    for cb in range(cbs):
        vis_ref[:, cb * LANES : (cb + 1) * LANES] = data[cb, 0 : vis_ref.shape[0], :].astype(jnp.bfloat16)


def total_kernel(meta, each, back_ref, out_ref):
    near, high, _ = out_ref.shape
    rows = back_ref.shape[0]
    at = lax.rem(lax.broadcasted_iota(jnp.int32, (high, rows), 1), meta + 2 * each) - meta
    which = lax.broadcasted_iota(jnp.int32, (high, rows), 0)
    pick = jnp.where((which < each) & ((at == which) | (at == which + each)), 1.0, 0.0).astype(jnp.bfloat16)
    total = jnp.dot(pick, back_ref[...], preferred_element_type=jnp.float32)
    for i in range(near):
        out_ref[i] = total


def unpack_kernel(cap, part, slot_ref, back_ref, out_ref, data, rows):
    tiles = slot_ref.shape[0]
    cbs = out_ref.shape[1] // LANES
    data[...] = back_ref[...].astype(jnp.float32)

    def move(t, c):
        slot = slot_ref[t]
        d, r = slot // cap, lax.rem(slot, cap)
        for cb in range(cbs):
            at = d * part + cb * cap * POS + r * POS
            rows[cb, pl.ds(pl.multiple_of(t * POS, POS), POS), :] = data[pl.ds(at, POS), :]
        return c

    lax.fori_loop(0, tiles, move, 0, unroll=8)
    for cb in range(cbs):
        out_ref[:, cb * LANES : (cb + 1) * LANES] = rows[cb].astype(jnp.bfloat16)


def finish_kernel(each, parts_ref, gain_ref, shift_ref, scale_ref, out_ref):
    out_ref[...] = jnp.zeros_like(out_ref)
    n, taps = len(USED), out_ref.shape[0] - 4
    cbs = out_ref.shape[1] // LANES
    for cb in range(cbs):
        ch = slice(cb * LANES, (cb + 1) * LANES)

        def total(i):
            v = i * cbs + cb
            return parts_ref[v // each, v % each : v % each + 1, :]

        for i, tap in enumerate(USED):
            out_ref[tap : tap + 1, ch] = total(i)
        along, plain = total(n + 1), total(n + 2)
        out_ref[taps : taps + 1, ch] = total(n)
        out_ref[taps + 1 : taps + 2, ch] = along * scale_ref[:, ch]
        out_ref[taps + 2 : taps + 3, ch] = plain * scale_ref[:, ch]
        out_ref[taps + 3 : taps + 4, ch] = along * gain_ref[:, ch] + plain * shift_ref[:, ch]


ANY = pl.BlockSpec(memory_space=pl.ANY)
SMEM = pl.BlockSpec(memory_space=pltpu.SMEM)
VMEM = pl.BlockSpec(memory_space=pltpu.VMEM)


def call(kernel, ins, outs, scratch, out_specs):
    return pl.pallas_call(
        kernel,
        out_shape=outs,
        in_specs=ins,
        out_specs=out_specs,
        scratch_shapes=scratch,
        compiler_params=pltpu.CompilerParams(vmem_limit_bytes=VMEM_LIMIT),
    )


def per_device(tile_features, dw_kernel, dw_bias, ln_gain, ln_shift, layer_scale,
               sample_counts, tile_dest, tile_offset, seq_grad):
    tiles_dev, _, _, chans = tile_features.shape
    enc = lax.axis_size(ENC)
    width = float(chans * enc)
    peers = lax.axis_size(DP)
    cap = tiles_dev // peers + 1
    slots, cbs = peers * cap, chans // LANES
    blocks = seq_grad.shape[0] // POS
    near = lax.axis_size(NEAR)
    each = -(-ROWS * cbs // near)
    meta = cbs * cap * POS
    part, back_part = meta + 2, meta + 2 * each
    f32, i32, bf16 = jnp.float32, jnp.int32, jnp.bfloat16
    shape = jax.ShapeDtypeStruct
    bias, gain, shift, scale = (v.reshape(1, chans) for v in (dw_bias, ln_gain, ln_shift, layer_scale))

    def swap(v, axes):
        return lax.all_to_all(v, axes, split_axis=0, concat_axis=0, tiled=True)


    ints = jnp.concatenate([tile_dest, tile_offset, sample_counts], 1)
    send, slot = call(
        functools.partial(pack_kernel, peers, cap, part),
        [ANY, VMEM],
        (shape((peers * part, LANES), bf16), shape((tiles_dev,), i32)),
        [pltpu.VMEM((cbs, tiles_dev * POS, LANES), f32), pltpu.VMEM((peers * part, LANES), f32), pltpu.SMEM((peers,), i32),
         pltpu.SMEM(ints.shape, i32), pltpu.SemaphoreType.DMA],
        (VMEM, SMEM),
    )(ints, tile_features.reshape(tiles_dev * POS, chans))
    got = swap(send.reshape(peers, part // 2, 2, LANES), DP)
    data, ups, f, sums, off = call(
        functools.partial(conv_kernel, peers, cap, part),
        [VMEM] * 6,
        (
            shape((peers * part, LANES), f32),
            shape((cbs, slots * POS, LANES), f32),
            shape((cbs, POS, slots, LANES), f32),
            shape((enc, 4 * POS, slots), f32),
            shape((slots,), i32),
        ),
        [
            pltpu.VMEM((cbs, (blocks + 1) * POS, LANES), f32),
            pltpu.VMEM((slots, LANES), f32),
            pltpu.VMEM((8, LANES), i32),
            pltpu.VMEM((8, LANES), f32),
            pltpu.SMEM((8, LANES), i32),
            pltpu.SMEM((8, LANES), f32),
            pltpu.SemaphoreType.DMA((2,)),
        ],
        (VMEM, VMEM, VMEM, VMEM, SMEM),
    )(got.reshape(peers * part, LANES), seq_grad, dw_kernel, bias, gain, scale)
    sums = swap(sums, ENC)
    outgoing = call(
        functools.partial(grad_kernel, peers, near, cap, part, each, width),
        [VMEM] * 7,
        shape((peers * back_part, LANES), bf16),
        [
            pltpu.VMEM((slots, LANES), f32),
            pltpu.VMEM((peers * back_part, LANES), f32),
            pltpu.VMEM((ROWS, 8, chans), f32),
            pltpu.VMEM((near * each, LANES), f32),
        ],
        VMEM,
    )(sums, data, ups, f, dw_kernel, gain, scale)
    back = swap(outgoing.reshape(peers, back_part // 2, 2, LANES), DP).reshape(peers * back_part, LANES)
    vis = call(
        functools.partial(token_kernel, peers, cap, part, width),
        [SMEM] + [VMEM] * 6,
        shape((blocks * POS, chans), bf16),
        [
            pltpu.VMEM((slots, LANES), f32),
            pltpu.VMEM((cbs, slots * POS, LANES), f32),
            pltpu.VMEM((cbs, (blocks + 1) * POS, LANES), f32),
        ],
        VMEM,
    )(off, sums, data, f, gain, shift, scale)
    back, vis = lax.optimization_barrier((back, vis))
    mine = call(functools.partial(total_kernel, meta, each), [VMEM], shape((near, 8, LANES), f32), [], VMEM)(back)
    parts = swap(mine, NEAR)
    tile_grads = call(
        functools.partial(unpack_kernel, cap, back_part),
        [SMEM, VMEM],
        shape((tiles_dev * POS, chans), bf16),
        [pltpu.VMEM((peers * back_part, LANES), f32), pltpu.VMEM((cbs, tiles_dev * POS, LANES), f32)],
        VMEM,
    )(slot, back)
    param_grads = call(
        functools.partial(finish_kernel, each), [VMEM] * 4, shape((dw_kernel.shape[0] + 4, chans), f32), [], VMEM
    )(parts, gain, shift, scale)
    return vis, tile_grads.reshape(tile_features.shape), param_grads


def solution(mesh):
    grid = Mesh(mesh.devices.reshape(4, 4, 4, 4, 2), DP + ENC)
    placed = (
        P(DP, None, None, ENC),
        P(None, ENC),
        P(ENC),
        P(ENC),
        P(ENC),
        P(ENC),
        P(DP, None),
        P(DP, None),
        P(DP, None),
        P(DP, ENC),
    )
    return jax.shard_map(
        per_device,
        mesh=grid,
        in_specs=placed,
        out_specs=(P(DP, ENC), P(DP, None, None, ENC), P(None, ENC)),
        check_vma=False,
    )
```

```python
import functools

import jax
import jax.numpy as jnp
from jax import lax
from jax.experimental import pallas as pl
from jax.experimental.pallas import tpu as pltpu
from jax.sharding import Mesh
from jax.sharding import PartitionSpec as P

EPS = 1e-06
HGT, WID = 4, 2
POS = HGT * WID
LANES = 128
DP = ("zh", "zl", "y")
NEAR = ("zl", "y")
ENC = ("x", "core")
VMEM_LIMIT = 16 * 1024 * 1024


def full(a, b):
    (ha, wa), (hb, wb) = divmod(a, WID), divmod(b, WID)
    return (hb - ha + 3) * 7 + (wb - wa + 3)


USED = sorted({full(a, b) for a in range(POS) for b in range(POS)})
PLACE = {tap: i for i, tap in enumerate(USED)}
ROWS = len(USED) + 3


def pack_kernel(peers, cap, part, ints_hbm, tiles_ref, send_ref, slot_ref, rows, data, seen, ints, sem):
    fetch = pltpu.make_async_copy(ints_hbm, ints, sem)
    fetch.start()
    tiles = tiles_ref.shape[0] // POS
    cbs = tiles_ref.shape[1] // LANES
    meta = cbs * cap * POS
    data[...] = jnp.zeros_like(data)
    for cb in range(cbs):
        rows[cb] = tiles_ref[:, cb * LANES : (cb + 1) * LANES].astype(jnp.float32)

    def clear(i, c):
        seen[i] = 0
        return c

    lax.fori_loop(0, peers, clear, 0, unroll=8)
    fetch.wait()
    lane = lax.broadcasted_iota(jnp.int32, (1, LANES), 1)

    def move(t, carry):
        s, end = carry
        step = (t >= end).astype(jnp.int32)
        s = s + step
        count = ints[0, 2 * tiles + s]
        end = end + step * count
        d = ints[0, t]
        r = seen[d]
        seen[d] = r + 1
        slot_ref[t] = d * cap + r
        for cb in range(cbs):
            at = d * part + cb * cap * POS + r * POS
            data[pl.ds(at, POS), :] = rows[cb, pl.ds(pl.multiple_of(t * POS, POS), POS), :]
        note = jnp.where(lane == r, ints[0, tiles + t], jnp.where(lane == cap + r, count, 0))
        here = pl.ds(d * part + meta, 1)
        data[here, :] = data[here, :] + note.astype(jnp.float32)
        return s, end

    lax.fori_loop(0, tiles, move, (jnp.int32(0), ints[0, 2 * tiles]), unroll=4)
    send_ref[...] = data[...].astype(jnp.bfloat16)


def conv_kernel(peers, cap, part, got_ref, seq_ref, kern_ref, bias_ref, gain_ref, scale_ref,
                data, ups, f_ref, sums_ref, off_ref, seq, cols, off_v, wgt_v, off_s, wgt_s, sem):
    cbs = seq.shape[0]
    blocks = seq.shape[1] // POS - 1
    meta = cbs * cap * POS
    data[...] = got_ref[...].astype(jnp.float32)
    notes = data[pl.ds(meta, peers, stride=part), :]
    notes = jnp.concatenate([notes, jnp.zeros((LANES - peers, LANES), jnp.float32)], 0).T
    count = notes[cap : 2 * cap]
    off_v[0:cap] = jnp.where(count > 0.5, notes[0:cap], float(blocks)).astype(jnp.int32)
    wgt_v[0:cap] = jnp.where(count > 0.5, 8.0 / jnp.maximum(count, 1.0), 0.0)
    moves = [pltpu.make_async_copy(off_v, off_s, sem.at[0]), pltpu.make_async_copy(wgt_v, wgt_s, sem.at[1])]
    for m in moves:
        m.start()
    for cb in range(cbs):
        seq[cb, 0 : blocks * POS, :] = seq_ref[:, cb * LANES : (cb + 1) * LANES].astype(jnp.float32)
        seq[cb, blocks * POS :, :] = jnp.zeros((POS, LANES), jnp.float32)
    for m in moves:
        m.wait()
    for r in range(cap):

        def fetch(d, c, r=r):
            off, w = off_s[r, d], wgt_s[r, d]
            off_ref[r * peers + d] = off
            for cb in range(cbs):
                ups[cb, pl.ds(pl.multiple_of((r * peers + d) * POS, POS), POS), :] = (
                    seq[cb, pl.ds(pl.multiple_of(off * POS, POS), POS), :] * w
                )
            return c

        lax.fori_loop(0, peers, fetch, 0, unroll=32)
    lane = lax.broadcasted_iota(jnp.int32, (8, LANES), 1)
    for r in range(cap):

        def body(b, c, r=r):
            here = pl.ds(pl.multiple_of(r * peers + b * 8, 8), 8)
            xs = {}
            for cb in range(cbs):
                for q in range(POS):
                    xs[cb, q] = data[pl.ds(b * 8 * part + cb * cap * POS + r * POS + q, 8, stride=part), :]
            out = jnp.zeros((8, LANES), jnp.float32)
            for p in range(POS):
                tot = [None] * 4
                for cb in range(cbs):
                    ch = slice(cb * LANES, (cb + 1) * LANES)
                    f = bias_ref[:, ch] + kern_ref[full(p, 0) : full(p, 0) + 1, ch] * xs[cb, 0]
                    for q in range(1, POS):
                        f = f + kern_ref[full(p, q) : full(p, q) + 1, ch] * xs[cb, q]
                    f_ref[cb, p, here, :] = f
                    u = ups[cb, pl.ds((r * peers + b * 8) * POS + p, 8, stride=POS), :]
                    dn = u * (scale_ref[:, ch] * gain_ref[:, ch])
                    new = [f, f * f, dn, dn * f]
                    tot = new if cb == 0 else [a + n for a, n in zip(tot, new)]
                for k in range(4):
                    out = jnp.where(lane == k * POS + p, jnp.sum(tot[k], 1, keepdims=True), out)
            cols[here, :] = out
            return c

        lax.fori_loop(0, peers // 8, body, 0, unroll=8)
    total = cols[...].T[0 : 4 * POS]
    for i in range(sums_ref.shape[0]):
        sums_ref[i] = total


def stats_columns(sums_ref, width):
    sums = sums_ref[0]
    for i in range(1, sums_ref.shape[0]):
        sums = sums + sums_ref[i]
    center = sums[0:POS] / width
    inv = lax.rsqrt(jnp.maximum(sums[POS : 2 * POS] / width - center * center, 0.0) + EPS)
    first = sums[2 * POS : 3 * POS]
    second = inv * (sums[3 * POS : 4 * POS] - center * first)
    slope = -(inv * inv) * (second / width)
    base = -inv * (first / width) - slope * center
    slots = sums.shape[1]
    rows = [center, inv, base, slope, jnp.zeros((LANES - 4 * POS, slots), jnp.float32)]
    return jnp.concatenate(rows, 0).T


def grad_kernel(peers, near, cap, part, each, width, sums_ref, data_ref, ups_ref, f_ref, kern_ref, gain_ref, scale_ref,
                out_ref, stats, data, acc, partial):
    cbs = f_ref.shape[0]
    meta = cbs * cap * POS
    back = meta + 2 * each
    stats[...] = stats_columns(sums_ref, width)
    acc[...] = jnp.zeros_like(acc)
    for r in range(cap):

        def body(b, c, r=r):
            here = pl.ds(pl.multiple_of(r * peers + b * 8, 8), 8)
            st = stats[here, :]
            for cb in range(cbs):
                ch = slice(cb * LANES, (cb + 1) * LANES)

                def add(row, v):
                    acc[row, :, ch] = acc[row, :, ch] + v

                df, xs, us = [], [], []
                a_sum = b_sum = d_sum = None
                for p in range(POS):
                    col = [st[:, k * POS + p : k * POS + p + 1] for k in range(4)]
                    u = ups_ref[cb, pl.ds((r * peers + b * 8) * POS + p, 8, stride=POS), :]
                    f = f_ref[cb, p, here, :]
                    w = u * col[1]
                    d = w * (scale_ref[:, ch] * gain_ref[:, ch]) + (f * col[3] + col[2])
                    along = w * (f - col[0])
                    df.append(d)
                    us.append(u)
                    xs.append(data_ref[pl.ds(b * 8 * part + cb * cap * POS + r * POS + p, 8, stride=part), :])
                    a_sum = along if p == 0 else a_sum + along
                    b_sum = u if p == 0 else b_sum + u
                    d_sum = d if p == 0 else d_sum + d
                taps = {}
                for p in range(POS):
                    for q in range(POS):
                        t = PLACE[full(p, q)]
                        v = df[p] * xs[q]
                        taps[t] = v if t not in taps else taps[t] + v
                for t, v in taps.items():
                    add(t, v)
                add(len(USED), d_sum)
                add(len(USED) + 1, a_sum)
                add(len(USED) + 2, b_sum)
                for q in range(POS):
                    t = us[q]
                    for p in range(POS):
                        t = t + kern_ref[full(p, q) : full(p, q) + 1, ch] * df[p]
                    data[pl.ds(b * 8 * back + cb * cap * POS + r * POS + q, 8, stride=back), :] = t
            return c

        lax.fori_loop(0, peers // 8, body, 0, unroll=8)
    for row in range(ROWS):
        for cb in range(cbs):
            v = row * cbs + cb
            partial[v : v + 1, :] = jnp.sum(acc[row, :, cb * LANES : (cb + 1) * LANES], 0, keepdims=True)
    partial[ROWS * cbs :, :] = jnp.zeros((each * near - ROWS * cbs, LANES), jnp.float32)
    for i in range(each):
        sums = partial[pl.ds(i, near, stride=each), :]
        high = sums.astype(jnp.bfloat16).astype(jnp.float32)
        for j, v in ((i, high), (i + each, sums - high)):
            for far in range(peers // near):
                data[pl.ds(far * near * back + meta + j, near, stride=back), :] = v
    out_ref[...] = data[...].astype(jnp.bfloat16)


def token_kernel(peers, cap, part, width, off_ref, sums_ref, data_ref, f_ref, gain_ref, shift_ref, scale_ref,
                 vis_ref, stats, toks, data):
    cbs = f_ref.shape[0]
    slots = peers * cap
    stats[...] = stats_columns(sums_ref, width)
    data[...] = jnp.zeros_like(data)
    for r in range(cap):

        def body(b, c, r=r):
            here = pl.ds(pl.multiple_of(r * peers + b * 8, 8), 8)
            st = stats[here, :]
            for cb in range(cbs):
                ch = slice(cb * LANES, (cb + 1) * LANES)
                for p in range(POS):
                    n = (f_ref[cb, p, here, :] - st[:, p : p + 1]) * st[:, POS + p : POS + p + 1]
                    m = n * gain_ref[:, ch] + shift_ref[:, ch]
                    x = data_ref[pl.ds(b * 8 * part + cb * cap * POS + r * POS + p, 8, stride=part), :]
                    toks[cb, pl.ds((r * peers + b * 8) * POS + p, 8, stride=POS), :] = x + scale_ref[:, ch] * m
            return c

        lax.fori_loop(0, peers // 8, body, 0)

    def put(s, c):
        at = pl.ds(pl.multiple_of(off_ref[s] * POS, POS), POS)
        for cb in range(cbs):
            data[cb, at, :] = toks[cb, pl.ds(pl.multiple_of(s * POS, POS), POS), :]
        return c

    lax.fori_loop(0, slots, put, 0, unroll=8)
    for cb in range(cbs):
        vis_ref[:, cb * LANES : (cb + 1) * LANES] = data[cb, 0 : vis_ref.shape[0], :].astype(jnp.bfloat16)


def total_kernel(meta, each, back_ref, out_ref):
    near, high, _ = out_ref.shape
    rows = back_ref.shape[0]
    at = lax.rem(lax.broadcasted_iota(jnp.int32, (high, rows), 1), meta + 2 * each) - meta
    which = lax.broadcasted_iota(jnp.int32, (high, rows), 0)
    pick = jnp.where((which < each) & ((at == which) | (at == which + each)), 1.0, 0.0).astype(jnp.bfloat16)
    total = jnp.dot(pick, back_ref[...], preferred_element_type=jnp.float32)
    for i in range(near):
        out_ref[i] = total


def unpack_kernel(cap, part, slot_ref, back_ref, out_ref, data, rows):
    tiles = slot_ref.shape[0]
    cbs = out_ref.shape[1] // LANES
    data[...] = back_ref[...].astype(jnp.float32)

    def move(t, c):
        slot = slot_ref[t]
        d, r = slot // cap, lax.rem(slot, cap)
        for cb in range(cbs):
            at = d * part + cb * cap * POS + r * POS
            rows[cb, pl.ds(pl.multiple_of(t * POS, POS), POS), :] = data[pl.ds(at, POS), :]
        return c

    lax.fori_loop(0, tiles, move, 0, unroll=8)
    for cb in range(cbs):
        out_ref[:, cb * LANES : (cb + 1) * LANES] = rows[cb].astype(jnp.bfloat16)


def finish_kernel(each, parts_ref, gain_ref, shift_ref, scale_ref, out_ref):
    out_ref[...] = jnp.zeros_like(out_ref)
    n, taps = len(USED), out_ref.shape[0] - 4
    cbs = out_ref.shape[1] // LANES
    for cb in range(cbs):
        ch = slice(cb * LANES, (cb + 1) * LANES)

        def total(i):
            v = i * cbs + cb
            return parts_ref[v // each, v % each : v % each + 1, :]

        for i, tap in enumerate(USED):
            out_ref[tap : tap + 1, ch] = total(i)
        along, plain = total(n + 1), total(n + 2)
        out_ref[taps : taps + 1, ch] = total(n)
        out_ref[taps + 1 : taps + 2, ch] = along * scale_ref[:, ch]
        out_ref[taps + 2 : taps + 3, ch] = plain * scale_ref[:, ch]
        out_ref[taps + 3 : taps + 4, ch] = along * gain_ref[:, ch] + plain * shift_ref[:, ch]


ANY = pl.BlockSpec(memory_space=pl.ANY)
SMEM = pl.BlockSpec(memory_space=pltpu.SMEM)
VMEM = pl.BlockSpec(memory_space=pltpu.VMEM)


def call(kernel, ins, outs, scratch, out_specs):
    return pl.pallas_call(
        kernel,
        out_shape=outs,
        in_specs=ins,
        out_specs=out_specs,
        scratch_shapes=scratch,
        compiler_params=pltpu.CompilerParams(vmem_limit_bytes=VMEM_LIMIT),
    )


def per_device(tile_features, dw_kernel, dw_bias, ln_gain, ln_shift, layer_scale,
               sample_counts, tile_dest, tile_offset, seq_grad):
    tiles_dev, _, _, chans = tile_features.shape
    enc = lax.axis_size(ENC)
    width = float(chans * enc)
    peers = lax.axis_size(DP)
    cap = tiles_dev // peers + 1
    slots, cbs = peers * cap, chans // LANES
    blocks = seq_grad.shape[0] // POS
    near = lax.axis_size(NEAR)
    each = -(-ROWS * cbs // near)
    meta = cbs * cap * POS
    part, back_part = meta + 2, meta + 2 * each
    f32, i32, bf16 = jnp.float32, jnp.int32, jnp.bfloat16
    shape = jax.ShapeDtypeStruct
    bias, gain, shift, scale = (v.reshape(1, chans) for v in (dw_bias, ln_gain, ln_shift, layer_scale))

    def swap(v, axes):
        return lax.all_to_all(v, axes, split_axis=0, concat_axis=0, tiled=True)


    ints = jnp.concatenate([tile_dest, tile_offset, sample_counts], 1)
    send, slot = call(
        functools.partial(pack_kernel, peers, cap, part),
        [ANY, VMEM],
        (shape((peers * part, LANES), bf16), shape((tiles_dev,), i32)),
        [pltpu.VMEM((cbs, tiles_dev * POS, LANES), f32), pltpu.VMEM((peers * part, LANES), f32), pltpu.SMEM((peers,), i32),
         pltpu.SMEM(ints.shape, i32), pltpu.SemaphoreType.DMA],
        (VMEM, SMEM),
    )(ints, tile_features.reshape(tiles_dev * POS, chans))
    got = swap(send.reshape(peers, part // 2, 2, LANES), DP)
    data, ups, f, sums, off = call(
        functools.partial(conv_kernel, peers, cap, part),
        [VMEM] * 6,
        (
            shape((peers * part, LANES), f32),
            shape((cbs, slots * POS, LANES), f32),
            shape((cbs, POS, slots, LANES), f32),
            shape((enc, 4 * POS, slots), f32),
            shape((slots,), i32),
        ),
        [
            pltpu.VMEM((cbs, (blocks + 1) * POS, LANES), f32),
            pltpu.VMEM((slots, LANES), f32),
            pltpu.VMEM((8, LANES), i32),
            pltpu.VMEM((8, LANES), f32),
            pltpu.SMEM((8, LANES), i32),
            pltpu.SMEM((8, LANES), f32),
            pltpu.SemaphoreType.DMA((2,)),
        ],
        (VMEM, VMEM, VMEM, VMEM, SMEM),
    )(got.reshape(peers * part, LANES), seq_grad, dw_kernel, bias, gain, scale)
    sums = swap(sums, ENC)
    outgoing = call(
        functools.partial(grad_kernel, peers, near, cap, part, each, width),
        [VMEM] * 7,
        shape((peers * back_part, LANES), bf16),
        [
            pltpu.VMEM((slots, LANES), f32),
            pltpu.VMEM((peers * back_part, LANES), f32),
            pltpu.VMEM((ROWS, 8, chans), f32),
            pltpu.VMEM((near * each, LANES), f32),
        ],
        VMEM,
    )(sums, data, ups, f, dw_kernel, gain, scale)
    back = swap(outgoing.reshape(peers, back_part // 2, 2, LANES), DP).reshape(peers * back_part, LANES)
    vis = call(
        functools.partial(token_kernel, peers, cap, part, width),
        [SMEM] + [VMEM] * 6,
        shape((blocks * POS, chans), bf16),
        [
            pltpu.VMEM((slots, LANES), f32),
            pltpu.VMEM((cbs, slots * POS, LANES), f32),
            pltpu.VMEM((cbs, (blocks + 1) * POS, LANES), f32),
        ],
        VMEM,
    )(off, sums, data, f, gain, shift, scale)
    back, vis = lax.optimization_barrier((back, vis))
    mine = call(functools.partial(total_kernel, meta, each), [VMEM], shape((near, 8, LANES), f32), [], VMEM)(back)
    parts = swap(mine, NEAR)
    tile_grads = call(
        functools.partial(unpack_kernel, cap, back_part),
        [SMEM, VMEM],
        shape((tiles_dev * POS, chans), bf16),
        [pltpu.VMEM((peers * back_part, LANES), f32), pltpu.VMEM((cbs, tiles_dev * POS, LANES), f32)],
        VMEM,
    )(slot, back)
    param_grads = call(
        functools.partial(finish_kernel, each), [VMEM] * 4, shape((dw_kernel.shape[0] + 4, chans), f32), [], VMEM
    )(parts, gain, shift, scale)
    return vis, tile_grads.reshape(tile_features.shape), param_grads


def solution(mesh):
    grid = Mesh(mesh.devices.reshape(4, 4, 4, 4, 2), DP + ENC)
    placed = (
        P(DP, None, None, ENC),
        P(None, ENC),
        P(ENC),
        P(ENC),
        P(ENC),
        P(ENC),
        P(DP, None),
        P(DP, None),
        P(DP, None),
        P(DP, ENC),
    )
    return jax.shard_map(
        per_device,
        mesh=grid,
        in_specs=placed,
        out_specs=(P(DP, ENC), P(DP, None, None, ENC), P(None, ENC)),
        check_vma=False,
    )
```

```python
import functools

import jax
import jax.numpy as jnp
from jax import lax
from jax.experimental import pallas as pl
from jax.experimental.pallas import tpu as pltpu
from jax.sharding import Mesh
from jax.sharding import PartitionSpec as P

EPS = 1e-06
HGT, WID = 4, 2
POS = HGT * WID
LANES = 128
DP = ("zh", "zl", "y")
NEAR = ("zl", "y")
ENC = ("x", "core")
VMEM_LIMIT = 16 * 1024 * 1024


def full(a, b):
    (ha, wa), (hb, wb) = divmod(a, WID), divmod(b, WID)
    return (hb - ha + 3) * 7 + (wb - wa + 3)


USED = sorted({full(a, b) for a in range(POS) for b in range(POS)})
PLACE = {tap: i for i, tap in enumerate(USED)}
ROWS = len(USED) + 3


def pack_kernel(peers, cap, part, ints_hbm, tiles_ref, send_ref, slot_ref, rows, data, seen, ints, sem):
    fetch = pltpu.make_async_copy(ints_hbm, ints, sem)
    fetch.start()
    tiles = tiles_ref.shape[0] // POS
    cbs = tiles_ref.shape[1] // LANES
    meta = cbs * cap * POS
    data[...] = jnp.zeros_like(data)
    for cb in range(cbs):
        rows[cb] = tiles_ref[:, cb * LANES : (cb + 1) * LANES].astype(jnp.float32)

    def clear(i, c):
        seen[i] = 0
        return c

    lax.fori_loop(0, peers, clear, 0, unroll=8)
    fetch.wait()
    lane = lax.broadcasted_iota(jnp.int32, (1, LANES), 1)

    def move(t, carry):
        s, end = carry
        step = (t >= end).astype(jnp.int32)
        s = s + step
        count = ints[0, 2 * tiles + s]
        end = end + step * count
        d = ints[0, t]
        r = seen[d]
        seen[d] = r + 1
        slot_ref[t] = d * cap + r
        for cb in range(cbs):
            at = d * part + cb * cap * POS + r * POS
            data[pl.ds(at, POS), :] = rows[cb, pl.ds(pl.multiple_of(t * POS, POS), POS), :]
        note = jnp.where(lane == r, ints[0, tiles + t], jnp.where(lane == cap + r, count, 0))
        here = pl.ds(d * part + meta, 1)
        data[here, :] = data[here, :] + note.astype(jnp.float32)
        return s, end

    lax.fori_loop(0, tiles, move, (jnp.int32(0), ints[0, 2 * tiles]), unroll=16)
    send_ref[...] = data[...].astype(jnp.bfloat16)


def conv_kernel(peers, cap, part, got_ref, seq_ref, kern_ref, bias_ref, gain_ref, scale_ref,
                data, ups, f_ref, sums_ref, off_ref, seq, cols, off_v, wgt_v, off_s, wgt_s, sem):
    cbs = seq.shape[0]
    blocks = seq.shape[1] // POS - 1
    meta = cbs * cap * POS
    data[...] = got_ref[...].astype(jnp.float32)
    notes = data[pl.ds(meta, peers, stride=part), :]
    notes = jnp.concatenate([notes, jnp.zeros((LANES - peers, LANES), jnp.float32)], 0).T
    count = notes[cap : 2 * cap]
    off_v[0:cap] = jnp.where(count > 0.5, notes[0:cap], float(blocks)).astype(jnp.int32)
    wgt_v[0:cap] = jnp.where(count > 0.5, 8.0 / jnp.maximum(count, 1.0), 0.0)
    moves = [pltpu.make_async_copy(off_v, off_s, sem.at[0]), pltpu.make_async_copy(wgt_v, wgt_s, sem.at[1])]
    for m in moves:
        m.start()
    for cb in range(cbs):
        seq[cb, 0 : blocks * POS, :] = seq_ref[:, cb * LANES : (cb + 1) * LANES].astype(jnp.float32)
        seq[cb, blocks * POS :, :] = jnp.zeros((POS, LANES), jnp.float32)
    for m in moves:
        m.wait()
    for r in range(cap):

        def fetch(d, c, r=r):
            off, w = off_s[r, d], wgt_s[r, d]
            off_ref[r * peers + d] = off
            for cb in range(cbs):
                ups[cb, pl.ds(pl.multiple_of((r * peers + d) * POS, POS), POS), :] = (
                    seq[cb, pl.ds(pl.multiple_of(off * POS, POS), POS), :] * w
                )
            return c

        lax.fori_loop(0, peers, fetch, 0, unroll=32)
    lane = lax.broadcasted_iota(jnp.int32, (8, LANES), 1)
    for r in range(cap):

        def body(b, c, r=r):
            here = pl.ds(pl.multiple_of(r * peers + b * 8, 8), 8)
            xs = {}
            for cb in range(cbs):
                for q in range(POS):
                    xs[cb, q] = data[pl.ds(b * 8 * part + cb * cap * POS + r * POS + q, 8, stride=part), :]
            out = jnp.zeros((8, LANES), jnp.float32)
            for p in range(POS):
                tot = [None] * 4
                for cb in range(cbs):
                    ch = slice(cb * LANES, (cb + 1) * LANES)
                    f = bias_ref[:, ch] + kern_ref[full(p, 0) : full(p, 0) + 1, ch] * xs[cb, 0]
                    for q in range(1, POS):
                        f = f + kern_ref[full(p, q) : full(p, q) + 1, ch] * xs[cb, q]
                    f_ref[cb, p, here, :] = f
                    u = ups[cb, pl.ds((r * peers + b * 8) * POS + p, 8, stride=POS), :]
                    dn = u * (scale_ref[:, ch] * gain_ref[:, ch])
                    new = [f, f * f, dn, dn * f]
                    tot = new if cb == 0 else [a + n for a, n in zip(tot, new)]
                for k in range(4):
                    out = jnp.where(lane == k * POS + p, jnp.sum(tot[k], 1, keepdims=True), out)
            cols[here, :] = out
            return c

        lax.fori_loop(0, peers // 8, body, 0, unroll=8)
    total = cols[...].T[0 : 4 * POS]
    for i in range(sums_ref.shape[0]):
        sums_ref[i] = total


def stats_columns(sums_ref, width):
    sums = sums_ref[0]
    for i in range(1, sums_ref.shape[0]):
        sums = sums + sums_ref[i]
    center = sums[0:POS] / width
    inv = lax.rsqrt(jnp.maximum(sums[POS : 2 * POS] / width - center * center, 0.0) + EPS)
    first = sums[2 * POS : 3 * POS]
    second = inv * (sums[3 * POS : 4 * POS] - center * first)
    slope = -(inv * inv) * (second / width)
    base = -inv * (first / width) - slope * center
    slots = sums.shape[1]
    rows = [center, inv, base, slope, jnp.zeros((LANES - 4 * POS, slots), jnp.float32)]
    return jnp.concatenate(rows, 0).T


def grad_kernel(peers, near, cap, part, each, width, sums_ref, data_ref, ups_ref, f_ref, kern_ref, gain_ref, scale_ref,
                out_ref, stats, data, acc, partial):
    cbs = f_ref.shape[0]
    meta = cbs * cap * POS
    back = meta + 2 * each
    stats[...] = stats_columns(sums_ref, width)
    acc[...] = jnp.zeros_like(acc)
    for r in range(cap):

        def body(b, c, r=r):
            here = pl.ds(pl.multiple_of(r * peers + b * 8, 8), 8)
            st = stats[here, :]
            for cb in range(cbs):
                ch = slice(cb * LANES, (cb + 1) * LANES)

                def add(row, v):
                    acc[row, :, ch] = acc[row, :, ch] + v

                df, xs, us = [], [], []
                a_sum = b_sum = d_sum = None
                for p in range(POS):
                    col = [st[:, k * POS + p : k * POS + p + 1] for k in range(4)]
                    u = ups_ref[cb, pl.ds((r * peers + b * 8) * POS + p, 8, stride=POS), :]
                    f = f_ref[cb, p, here, :]
                    w = u * col[1]
                    d = w * (scale_ref[:, ch] * gain_ref[:, ch]) + (f * col[3] + col[2])
                    along = w * (f - col[0])
                    df.append(d)
                    us.append(u)
                    xs.append(data_ref[pl.ds(b * 8 * part + cb * cap * POS + r * POS + p, 8, stride=part), :])
                    a_sum = along if p == 0 else a_sum + along
                    b_sum = u if p == 0 else b_sum + u
                    d_sum = d if p == 0 else d_sum + d
                taps = {}
                for p in range(POS):
                    for q in range(POS):
                        t = PLACE[full(p, q)]
                        v = df[p] * xs[q]
                        taps[t] = v if t not in taps else taps[t] + v
                for t, v in taps.items():
                    add(t, v)
                add(len(USED), d_sum)
                add(len(USED) + 1, a_sum)
                add(len(USED) + 2, b_sum)
                for q in range(POS):
                    t = us[q]
                    for p in range(POS):
                        t = t + kern_ref[full(p, q) : full(p, q) + 1, ch] * df[p]
                    data[pl.ds(b * 8 * back + cb * cap * POS + r * POS + q, 8, stride=back), :] = t
            return c

        lax.fori_loop(0, peers // 8, body, 0, unroll=8)
    for row in range(ROWS):
        for cb in range(cbs):
            v = row * cbs + cb
            partial[v : v + 1, :] = jnp.sum(acc[row, :, cb * LANES : (cb + 1) * LANES], 0, keepdims=True)
    partial[ROWS * cbs :, :] = jnp.zeros((each * near - ROWS * cbs, LANES), jnp.float32)
    for i in range(each):
        sums = partial[pl.ds(i, near, stride=each), :]
        high = sums.astype(jnp.bfloat16).astype(jnp.float32)
        for j, v in ((i, high), (i + each, sums - high)):
            for far in range(peers // near):
                data[pl.ds(far * near * back + meta + j, near, stride=back), :] = v
    out_ref[...] = data[...].astype(jnp.bfloat16)


def token_kernel(peers, cap, part, width, off_ref, sums_ref, data_ref, f_ref, gain_ref, shift_ref, scale_ref,
                 vis_ref, stats, toks, data):
    cbs = f_ref.shape[0]
    slots = peers * cap
    stats[...] = stats_columns(sums_ref, width)
    data[...] = jnp.zeros_like(data)
    for r in range(cap):

        def body(b, c, r=r):
            here = pl.ds(pl.multiple_of(r * peers + b * 8, 8), 8)
            st = stats[here, :]
            for cb in range(cbs):
                ch = slice(cb * LANES, (cb + 1) * LANES)
                for p in range(POS):
                    n = (f_ref[cb, p, here, :] - st[:, p : p + 1]) * st[:, POS + p : POS + p + 1]
                    m = n * gain_ref[:, ch] + shift_ref[:, ch]
                    x = data_ref[pl.ds(b * 8 * part + cb * cap * POS + r * POS + p, 8, stride=part), :]
                    toks[cb, pl.ds((r * peers + b * 8) * POS + p, 8, stride=POS), :] = x + scale_ref[:, ch] * m
            return c

        lax.fori_loop(0, peers // 8, body, 0, unroll=8)

    def put(s, c):
        at = pl.ds(pl.multiple_of(off_ref[s] * POS, POS), POS)
        for cb in range(cbs):
            data[cb, at, :] = toks[cb, pl.ds(pl.multiple_of(s * POS, POS), POS), :]
        return c

    lax.fori_loop(0, slots, put, 0, unroll=32)
    for cb in range(cbs):
        vis_ref[:, cb * LANES : (cb + 1) * LANES] = data[cb, 0 : vis_ref.shape[0], :].astype(jnp.bfloat16)


def total_kernel(meta, each, back_ref, out_ref):
    near, high, _ = out_ref.shape
    rows = back_ref.shape[0]
    at = lax.rem(lax.broadcasted_iota(jnp.int32, (high, rows), 1), meta + 2 * each) - meta
    which = lax.broadcasted_iota(jnp.int32, (high, rows), 0)
    pick = jnp.where((which < each) & ((at == which) | (at == which + each)), 1.0, 0.0).astype(jnp.bfloat16)
    total = jnp.dot(pick, back_ref[...], preferred_element_type=jnp.float32)
    for i in range(near):
        out_ref[i] = total


def unpack_kernel(cap, part, slot_ref, back_ref, out_ref, data, rows):
    tiles = slot_ref.shape[0]
    cbs = out_ref.shape[1] // LANES
    data[...] = back_ref[...].astype(jnp.float32)

    def move(t, c):
        slot = slot_ref[t]
        d, r = slot // cap, lax.rem(slot, cap)
        for cb in range(cbs):
            at = d * part + cb * cap * POS + r * POS
            rows[cb, pl.ds(pl.multiple_of(t * POS, POS), POS), :] = data[pl.ds(at, POS), :]
        return c

    lax.fori_loop(0, tiles, move, 0, unroll=32)
    for cb in range(cbs):
        out_ref[:, cb * LANES : (cb + 1) * LANES] = rows[cb].astype(jnp.bfloat16)


def finish_kernel(each, parts_ref, gain_ref, shift_ref, scale_ref, out_ref):
    out_ref[...] = jnp.zeros_like(out_ref)
    n, taps = len(USED), out_ref.shape[0] - 4
    cbs = out_ref.shape[1] // LANES
    for cb in range(cbs):
        ch = slice(cb * LANES, (cb + 1) * LANES)

        def total(i):
            v = i * cbs + cb
            return parts_ref[v // each, v % each : v % each + 1, :]

        for i, tap in enumerate(USED):
            out_ref[tap : tap + 1, ch] = total(i)
        along, plain = total(n + 1), total(n + 2)
        out_ref[taps : taps + 1, ch] = total(n)
        out_ref[taps + 1 : taps + 2, ch] = along * scale_ref[:, ch]
        out_ref[taps + 2 : taps + 3, ch] = plain * scale_ref[:, ch]
        out_ref[taps + 3 : taps + 4, ch] = along * gain_ref[:, ch] + plain * shift_ref[:, ch]


ANY = pl.BlockSpec(memory_space=pl.ANY)
SMEM = pl.BlockSpec(memory_space=pltpu.SMEM)
VMEM = pl.BlockSpec(memory_space=pltpu.VMEM)


def call(kernel, ins, outs, scratch, out_specs):
    return pl.pallas_call(
        kernel,
        out_shape=outs,
        in_specs=ins,
        out_specs=out_specs,
        scratch_shapes=scratch,
        compiler_params=pltpu.CompilerParams(vmem_limit_bytes=VMEM_LIMIT),
    )


def per_device(tile_features, dw_kernel, dw_bias, ln_gain, ln_shift, layer_scale,
               sample_counts, tile_dest, tile_offset, seq_grad):
    tiles_dev, _, _, chans = tile_features.shape
    enc = lax.axis_size(ENC)
    width = float(chans * enc)
    peers = lax.axis_size(DP)
    cap = tiles_dev // peers + 1
    slots, cbs = peers * cap, chans // LANES
    blocks = seq_grad.shape[0] // POS
    near = lax.axis_size(NEAR)
    each = -(-ROWS * cbs // near)
    meta = cbs * cap * POS
    part, back_part = meta + 2, meta + 2 * each
    f32, i32, bf16 = jnp.float32, jnp.int32, jnp.bfloat16
    shape = jax.ShapeDtypeStruct
    bias, gain, shift, scale = (v.reshape(1, chans) for v in (dw_bias, ln_gain, ln_shift, layer_scale))

    def swap(v, axes):
        return lax.all_to_all(v, axes, split_axis=0, concat_axis=0, tiled=True)


    ints = jnp.concatenate([tile_dest, tile_offset, sample_counts], 1)
    send, slot = call(
        functools.partial(pack_kernel, peers, cap, part),
        [ANY, VMEM],
        (shape((peers * part, LANES), bf16), shape((tiles_dev,), i32)),
        [pltpu.VMEM((cbs, tiles_dev * POS, LANES), f32), pltpu.VMEM((peers * part, LANES), f32), pltpu.SMEM((peers,), i32),
         pltpu.SMEM(ints.shape, i32), pltpu.SemaphoreType.DMA],
        (VMEM, SMEM),
    )(ints, tile_features.reshape(tiles_dev * POS, chans))
    got = swap(send.reshape(peers, part // 2, 2, LANES), DP)
    data, ups, f, sums, off = call(
        functools.partial(conv_kernel, peers, cap, part),
        [VMEM] * 6,
        (
            shape((peers * part, LANES), f32),
            shape((cbs, slots * POS, LANES), f32),
            shape((cbs, POS, slots, LANES), f32),
            shape((enc, 4 * POS, slots), f32),
            shape((slots,), i32),
        ),
        [
            pltpu.VMEM((cbs, (blocks + 1) * POS, LANES), f32),
            pltpu.VMEM((slots, LANES), f32),
            pltpu.VMEM((8, LANES), i32),
            pltpu.VMEM((8, LANES), f32),
            pltpu.SMEM((8, LANES), i32),
            pltpu.SMEM((8, LANES), f32),
            pltpu.SemaphoreType.DMA((2,)),
        ],
        (VMEM, VMEM, VMEM, VMEM, SMEM),
    )(got.reshape(peers * part, LANES), seq_grad, dw_kernel, bias, gain, scale)
    sums = swap(sums, ENC)
    outgoing = call(
        functools.partial(grad_kernel, peers, near, cap, part, each, width),
        [VMEM] * 7,
        shape((peers * back_part, LANES), bf16),
        [
            pltpu.VMEM((slots, LANES), f32),
            pltpu.VMEM((peers * back_part, LANES), f32),
            pltpu.VMEM((ROWS, 8, chans), f32),
            pltpu.VMEM((near * each, LANES), f32),
        ],
        VMEM,
    )(sums, data, ups, f, dw_kernel, gain, scale)
    back = swap(outgoing.reshape(peers, back_part // 2, 2, LANES), DP).reshape(peers * back_part, LANES)
    vis = call(
        functools.partial(token_kernel, peers, cap, part, width),
        [SMEM] + [VMEM] * 6,
        shape((blocks * POS, chans), bf16),
        [
            pltpu.VMEM((slots, LANES), f32),
            pltpu.VMEM((cbs, slots * POS, LANES), f32),
            pltpu.VMEM((cbs, (blocks + 1) * POS, LANES), f32),
        ],
        VMEM,
    )(off, sums, data, f, gain, shift, scale)
    mine = call(functools.partial(total_kernel, meta, each), [VMEM], shape((near, 8, LANES), f32), [], VMEM)(back)
    parts = swap(mine, NEAR)
    tile_grads = call(
        functools.partial(unpack_kernel, cap, back_part),
        [SMEM, VMEM],
        shape((tiles_dev * POS, chans), bf16),
        [pltpu.VMEM((peers * back_part, LANES), f32), pltpu.VMEM((cbs, tiles_dev * POS, LANES), f32)],
        VMEM,
    )(slot, back)
    param_grads = call(
        functools.partial(finish_kernel, each), [VMEM] * 4, shape((dw_kernel.shape[0] + 4, chans), f32), [], VMEM
    )(parts, gain, shift, scale)
    return vis, tile_grads.reshape(tile_features.shape), param_grads


def solution(mesh):
    grid = Mesh(mesh.devices.reshape(4, 4, 4, 4, 2), DP + ENC)
    placed = (
        P(DP, None, None, ENC),
        P(None, ENC),
        P(ENC),
        P(ENC),
        P(ENC),
        P(ENC),
        P(DP, None),
        P(DP, None),
        P(DP, None),
        P(DP, ENC),
    )
    return jax.shard_map(
        per_device,
        mesh=grid,
        in_specs=placed,
        out_specs=(P(DP, ENC), P(DP, None, None, ENC), P(None, ENC)),
        check_vma=False,
    )
```

```python
import functools

import jax
import jax.numpy as jnp
from jax import lax
from jax.experimental import pallas as pl
from jax.experimental.pallas import tpu as pltpu
from jax.sharding import Mesh
from jax.sharding import PartitionSpec as P

EPS = 1e-06
HGT, WID = 4, 2
POS = HGT * WID
LANES = 128
DP = ("zh", "zl", "y")
NEAR = ("zl", "y")
ENC = ("x", "core")
VMEM_LIMIT = 16 * 1024 * 1024


def full(a, b):
    (ha, wa), (hb, wb) = divmod(a, WID), divmod(b, WID)
    return (hb - ha + 3) * 7 + (wb - wa + 3)


USED = sorted({full(a, b) for a in range(POS) for b in range(POS)})
PLACE = {tap: i for i, tap in enumerate(USED)}
ROWS = len(USED) + 3


def pack_kernel(peers, cap, part, ints_hbm, tiles_ref, send_ref, slot_ref, rows, data, seen, ints, sem):
    fetch = pltpu.make_async_copy(ints_hbm, ints, sem)
    fetch.start()
    tiles = tiles_ref.shape[0] // POS
    cbs = tiles_ref.shape[1] // LANES
    meta = cbs * cap * POS
    data[...] = jnp.zeros_like(data)
    for cb in range(cbs):
        rows[cb] = tiles_ref[:, cb * LANES : (cb + 1) * LANES].astype(jnp.float32)

    def clear(i, c):
        seen[i] = 0
        return c

    lax.fori_loop(0, peers, clear, 0, unroll=8)
    fetch.wait()
    lane = lax.broadcasted_iota(jnp.int32, (1, LANES), 1)

    def move(t, carry):
        s, end = carry
        step = (t >= end).astype(jnp.int32)
        s = s + step
        count = ints[0, 2 * tiles + s]
        end = end + step * count
        d = ints[0, t]
        r = seen[d]
        seen[d] = r + 1
        slot_ref[t] = d * cap + r
        for cb in range(cbs):
            at = d * part + cb * cap * POS + r * POS
            data[pl.ds(at, POS), :] = rows[cb, pl.ds(pl.multiple_of(t * POS, POS), POS), :]
        note = jnp.where(lane == r, ints[0, tiles + t], jnp.where(lane == cap + r, count, 0))
        here = pl.ds(d * part + meta, 1)
        data[here, :] = data[here, :] + note.astype(jnp.float32)
        return s, end

    lax.fori_loop(0, tiles, move, (jnp.int32(0), ints[0, 2 * tiles]), unroll=16)
    send_ref[...] = data[...].astype(jnp.bfloat16)


def conv_kernel(peers, cap, part, got_ref, seq_ref, kern_ref, bias_ref, gain_ref, scale_ref,
                data, ups, f_ref, sums_ref, off_ref, both, seq, cols, off_v, wgt_v, off_s, wgt_s, sem):
    cbs = seq.shape[0]
    blocks = seq.shape[1] // POS - 1
    meta = cbs * cap * POS
    both[0:1, :] = (scale_ref[...] * gain_ref[...]).reshape(1, -1)
    both[1:2, :] = bias_ref[...].reshape(1, -1)
    data[...] = got_ref[...].astype(jnp.float32)
    notes = data[pl.ds(meta, peers, stride=part), :]
    notes = jnp.concatenate([notes, jnp.zeros((LANES - peers, LANES), jnp.float32)], 0).T
    count = notes[cap : 2 * cap]
    off_v[0:cap] = jnp.where(count > 0.5, notes[0:cap], float(blocks)).astype(jnp.int32)
    wgt_v[0:cap] = jnp.where(count > 0.5, 8.0 / jnp.maximum(count, 1.0), 0.0)
    moves = [pltpu.make_async_copy(off_v, off_s, sem.at[0]), pltpu.make_async_copy(wgt_v, wgt_s, sem.at[1])]
    for m in moves:
        m.start()
    for cb in range(cbs):
        seq[cb, 0 : blocks * POS, :] = seq_ref[:, cb * LANES : (cb + 1) * LANES].astype(jnp.float32)
        seq[cb, blocks * POS :, :] = jnp.zeros((POS, LANES), jnp.float32)
    for m in moves:
        m.wait()
    for r in range(cap):

        def fetch(d, c, r=r):
            off, w = off_s[r, d], wgt_s[r, d]
            off_ref[r * peers + d] = off
            for cb in range(cbs):
                ups[cb, pl.ds(pl.multiple_of((r * peers + d) * POS, POS), POS), :] = (
                    seq[cb, pl.ds(pl.multiple_of(off * POS, POS), POS), :] * w
                )
            return c

        lax.fori_loop(0, peers, fetch, 0, unroll=32)
    lane = lax.broadcasted_iota(jnp.int32, (8, LANES), 1)
    for r in range(cap):

        def body(b, c, r=r):
            here = pl.ds(pl.multiple_of(r * peers + b * 8, 8), 8)
            xs = {}
            for cb in range(cbs):
                for q in range(POS):
                    xs[cb, q] = data[pl.ds(b * 8 * part + cb * cap * POS + r * POS + q, 8, stride=part), :]
            out = jnp.zeros((8, LANES), jnp.float32)
            for p in range(POS):
                tot = [None] * 4
                for cb in range(cbs):
                    ch = slice(cb * LANES, (cb + 1) * LANES)
                    f = both[1:2, ch] + kern_ref[full(p, 0) : full(p, 0) + 1, ch] * xs[cb, 0]
                    for q in range(1, POS):
                        f = f + kern_ref[full(p, q) : full(p, q) + 1, ch] * xs[cb, q]
                    f_ref[cb, p, here, :] = f
                    u = ups[cb, pl.ds((r * peers + b * 8) * POS + p, 8, stride=POS), :]
                    dn = u * both[0:1, ch]
                    new = [f, f * f, dn, dn * f]
                    tot = new if cb == 0 else [a + n for a, n in zip(tot, new)]
                for k in range(4):
                    out = jnp.where(lane == k * POS + p, jnp.sum(tot[k], 1, keepdims=True), out)
            cols[here, :] = out
            return c

        lax.fori_loop(0, peers // 8, body, 0, unroll=8)
    total = cols[...].T[0 : 4 * POS]
    for i in range(sums_ref.shape[0]):
        sums_ref[i] = total


def stats_columns(sums_ref, width):
    sums = sums_ref[0]
    for i in range(1, sums_ref.shape[0]):
        sums = sums + sums_ref[i]
    center = sums[0:POS] / width
    inv = lax.rsqrt(jnp.maximum(sums[POS : 2 * POS] / width - center * center, 0.0) + EPS)
    first = sums[2 * POS : 3 * POS]
    second = inv * (sums[3 * POS : 4 * POS] - center * first)
    slope = -(inv * inv) * (second / width)
    base = -inv * (first / width) - slope * center
    slots = sums.shape[1]
    rows = [center, inv, base, slope, jnp.zeros((LANES - 4 * POS, slots), jnp.float32)]
    return jnp.concatenate(rows, 0).T


def grad_kernel(peers, near, cap, part, each, width, sums_ref, data_ref, ups_ref, f_ref, kern_ref, gain_ref, scale_ref,
                out_ref, both, stats, data, acc, partial):
    cbs = f_ref.shape[0]
    meta = cbs * cap * POS
    back = meta + 2 * each
    stats[...] = stats_columns(sums_ref, width)
    both[0:1, :] = (scale_ref[...] * gain_ref[...]).reshape(1, -1)
    acc[...] = jnp.zeros_like(acc)
    for r in range(cap):

        def body(b, c, r=r):
            here = pl.ds(pl.multiple_of(r * peers + b * 8, 8), 8)
            st = stats[here, :]
            for cb in range(cbs):
                ch = slice(cb * LANES, (cb + 1) * LANES)

                def add(row, v):
                    acc[row, :, ch] = acc[row, :, ch] + v

                df, xs, us = [], [], []
                a_sum = b_sum = d_sum = None
                for p in range(POS):
                    col = [st[:, k * POS + p : k * POS + p + 1] for k in range(4)]
                    u = ups_ref[cb, pl.ds((r * peers + b * 8) * POS + p, 8, stride=POS), :]
                    f = f_ref[cb, p, here, :]
                    w = u * col[1]
                    d = w * both[0:1, ch] + (f * col[3] + col[2])
                    along = w * (f - col[0])
                    df.append(d)
                    us.append(u)
                    xs.append(data_ref[pl.ds(b * 8 * part + cb * cap * POS + r * POS + p, 8, stride=part), :])
                    a_sum = along if p == 0 else a_sum + along
                    b_sum = u if p == 0 else b_sum + u
                    d_sum = d if p == 0 else d_sum + d
                taps = {}
                for p in range(POS):
                    for q in range(POS):
                        t = PLACE[full(p, q)]
                        v = df[p] * xs[q]
                        taps[t] = v if t not in taps else taps[t] + v
                for t, v in taps.items():
                    add(t, v)
                add(len(USED), d_sum)
                add(len(USED) + 1, a_sum)
                add(len(USED) + 2, b_sum)
                for q in range(POS):
                    t = us[q]
                    for p in range(POS):
                        t = t + kern_ref[full(p, q) : full(p, q) + 1, ch] * df[p]
                    data[pl.ds(b * 8 * back + cb * cap * POS + r * POS + q, 8, stride=back), :] = t
            return c

        lax.fori_loop(0, peers // 8, body, 0, unroll=8)
    for row in range(ROWS):
        for cb in range(cbs):
            v = row * cbs + cb
            partial[v : v + 1, :] = jnp.sum(acc[row, :, cb * LANES : (cb + 1) * LANES], 0, keepdims=True)
    partial[ROWS * cbs :, :] = jnp.zeros((each * near - ROWS * cbs, LANES), jnp.float32)
    for i in range(each):
        sums = partial[pl.ds(i, near, stride=each), :]
        high = sums.astype(jnp.bfloat16).astype(jnp.float32)
        for j, v in ((i, high), (i + each, sums - high)):
            for far in range(peers // near):
                data[pl.ds(far * near * back + meta + j, near, stride=back), :] = v
    out_ref[...] = data[...].astype(jnp.bfloat16)


def token_kernel(peers, cap, part, width, off_ref, sums_ref, data_ref, f_ref, gain_ref, shift_ref, scale_ref,
                 vis_ref, stats, toks, data):
    cbs = f_ref.shape[0]
    slots = peers * cap
    stats[...] = stats_columns(sums_ref, width)
    data[...] = jnp.zeros_like(data)
    for r in range(cap):

        def body(b, c, r=r):
            here = pl.ds(pl.multiple_of(r * peers + b * 8, 8), 8)
            st = stats[here, :]
            for cb in range(cbs):
                ch = slice(cb * LANES, (cb + 1) * LANES)
                for p in range(POS):
                    n = (f_ref[cb, p, here, :] - st[:, p : p + 1]) * st[:, POS + p : POS + p + 1]
                    m = n * gain_ref[ch] + shift_ref[ch]
                    x = data_ref[pl.ds(b * 8 * part + cb * cap * POS + r * POS + p, 8, stride=part), :]
                    toks[cb, pl.ds((r * peers + b * 8) * POS + p, 8, stride=POS), :] = x + scale_ref[ch] * m
            return c

        lax.fori_loop(0, peers // 8, body, 0, unroll=8)

    def put(s, c):
        at = pl.ds(pl.multiple_of(off_ref[s] * POS, POS), POS)
        for cb in range(cbs):
            data[cb, at, :] = toks[cb, pl.ds(pl.multiple_of(s * POS, POS), POS), :]
        return c

    lax.fori_loop(0, slots, put, 0, unroll=32)
    for cb in range(cbs):
        vis_ref[:, cb * LANES : (cb + 1) * LANES] = data[cb, 0 : vis_ref.shape[0], :].astype(jnp.bfloat16)


def total_kernel(meta, each, back_ref, out_ref):
    near, high, _ = out_ref.shape
    rows = back_ref.shape[0]
    at = lax.rem(lax.broadcasted_iota(jnp.int32, (high, rows), 1), meta + 2 * each) - meta
    which = lax.broadcasted_iota(jnp.int32, (high, rows), 0)
    pick = jnp.where((which < each) & ((at == which) | (at == which + each)), 1.0, 0.0).astype(jnp.bfloat16)
    total = jnp.dot(pick, back_ref[...], preferred_element_type=jnp.float32)
    for i in range(near):
        out_ref[i] = total


def unpack_kernel(cap, part, slot_ref, back_ref, out_ref, data, rows):
    tiles = slot_ref.shape[0]
    cbs = out_ref.shape[1] // LANES
    data[...] = back_ref[...].astype(jnp.float32)

    def move(t, c):
        slot = slot_ref[t]
        d, r = slot // cap, lax.rem(slot, cap)
        for cb in range(cbs):
            at = d * part + cb * cap * POS + r * POS
            rows[cb, pl.ds(pl.multiple_of(t * POS, POS), POS), :] = data[pl.ds(at, POS), :]
        return c

    lax.fori_loop(0, tiles, move, 0, unroll=32)
    for cb in range(cbs):
        out_ref[:, cb * LANES : (cb + 1) * LANES] = rows[cb].astype(jnp.bfloat16)


def finish_kernel(each, parts_ref, gain_ref, shift_ref, scale_ref, out_ref):
    out_ref[...] = jnp.zeros_like(out_ref)
    n, taps = len(USED), out_ref.shape[0] - 4
    cbs = out_ref.shape[1] // LANES
    for cb in range(cbs):
        ch = slice(cb * LANES, (cb + 1) * LANES)

        def total(i):
            v = i * cbs + cb
            return parts_ref[v // each, v % each : v % each + 1, :]

        for i, tap in enumerate(USED):
            out_ref[tap : tap + 1, ch] = total(i)
        along, plain = total(n + 1), total(n + 2)
        out_ref[taps : taps + 1, ch] = total(n)
        out_ref[taps + 1 : taps + 2, ch] = along * scale_ref[ch]
        out_ref[taps + 2 : taps + 3, ch] = plain * scale_ref[ch]
        out_ref[taps + 3 : taps + 4, ch] = along * gain_ref[ch] + plain * shift_ref[ch]


ANY = pl.BlockSpec(memory_space=pl.ANY)
SMEM = pl.BlockSpec(memory_space=pltpu.SMEM)
VMEM = pl.BlockSpec(memory_space=pltpu.VMEM)


def call(kernel, ins, outs, scratch, out_specs):
    return pl.pallas_call(
        kernel,
        out_shape=outs,
        in_specs=ins,
        out_specs=out_specs,
        scratch_shapes=scratch,
        compiler_params=pltpu.CompilerParams(vmem_limit_bytes=VMEM_LIMIT),
    )


def per_device(tile_features, dw_kernel, dw_bias, ln_gain, ln_shift, layer_scale,
               sample_counts, tile_dest, tile_offset, seq_grad):
    tiles_dev, _, _, chans = tile_features.shape
    enc = lax.axis_size(ENC)
    width = float(chans * enc)
    peers = lax.axis_size(DP)
    cap = tiles_dev // peers + 1
    slots, cbs = peers * cap, chans // LANES
    blocks = seq_grad.shape[0] // POS
    near = lax.axis_size(NEAR)
    each = -(-ROWS * cbs // near)
    meta = cbs * cap * POS
    part, back_part = meta + 2, meta + 2 * each
    f32, i32, bf16 = jnp.float32, jnp.int32, jnp.bfloat16
    shape = jax.ShapeDtypeStruct
    bias, gain, shift, scale = dw_bias, ln_gain, ln_shift, layer_scale

    def swap(v, axes):
        return lax.all_to_all(v, axes, split_axis=0, concat_axis=0, tiled=True)


    ints = jnp.concatenate([tile_dest, tile_offset, sample_counts], 1)
    send, slot = call(
        functools.partial(pack_kernel, peers, cap, part),
        [ANY, VMEM],
        (shape((peers * part, LANES), bf16), shape((tiles_dev,), i32)),
        [pltpu.VMEM((cbs, tiles_dev * POS, LANES), f32), pltpu.VMEM((peers * part, LANES), f32), pltpu.SMEM((peers,), i32),
         pltpu.SMEM(ints.shape, i32), pltpu.SemaphoreType.DMA],
        (VMEM, SMEM),
    )(ints, tile_features.reshape(tiles_dev * POS, chans))
    got = swap(send.reshape(peers, part // 2, 2, LANES), DP)
    data, ups, f, sums, off = call(
        functools.partial(conv_kernel, peers, cap, part),
        [VMEM] * 6,
        (
            shape((peers * part, LANES), f32),
            shape((cbs, slots * POS, LANES), f32),
            shape((cbs, POS, slots, LANES), f32),
            shape((enc, 4 * POS, slots), f32),
            shape((slots,), i32),
        ),
        [
            pltpu.VMEM((8, chans), f32),
            pltpu.VMEM((cbs, (blocks + 1) * POS, LANES), f32),
            pltpu.VMEM((slots, LANES), f32),
            pltpu.VMEM((8, LANES), i32),
            pltpu.VMEM((8, LANES), f32),
            pltpu.SMEM((8, LANES), i32),
            pltpu.SMEM((8, LANES), f32),
            pltpu.SemaphoreType.DMA((2,)),
        ],
        (VMEM, VMEM, VMEM, VMEM, SMEM),
    )(got.reshape(peers * part, LANES), seq_grad, dw_kernel, bias, gain, scale)
    sums = swap(sums, ENC)
    outgoing = call(
        functools.partial(grad_kernel, peers, near, cap, part, each, width),
        [VMEM] * 7,
        shape((peers * back_part, LANES), bf16),
        [
            pltpu.VMEM((8, chans), f32),
            pltpu.VMEM((slots, LANES), f32),
            pltpu.VMEM((peers * back_part, LANES), f32),
            pltpu.VMEM((ROWS, 8, chans), f32),
            pltpu.VMEM((near * each, LANES), f32),
        ],
        VMEM,
    )(sums, data, ups, f, dw_kernel, gain, scale)
    back = swap(outgoing.reshape(peers, back_part // 2, 2, LANES), DP).reshape(peers * back_part, LANES)
    vis = call(
        functools.partial(token_kernel, peers, cap, part, width),
        [SMEM] + [VMEM] * 6,
        shape((blocks * POS, chans), bf16),
        [
            pltpu.VMEM((slots, LANES), f32),
            pltpu.VMEM((cbs, slots * POS, LANES), f32),
            pltpu.VMEM((cbs, (blocks + 1) * POS, LANES), f32),
        ],
        VMEM,
    )(off, sums, data, f, gain, shift, scale)
    mine = call(functools.partial(total_kernel, meta, each), [VMEM], shape((near, 8, LANES), f32), [], VMEM)(back)
    parts = swap(mine, NEAR)
    tile_grads = call(
        functools.partial(unpack_kernel, cap, back_part),
        [SMEM, VMEM],
        shape((tiles_dev * POS, chans), bf16),
        [pltpu.VMEM((peers * back_part, LANES), f32), pltpu.VMEM((cbs, tiles_dev * POS, LANES), f32)],
        VMEM,
    )(slot, back)
    param_grads = call(
        functools.partial(finish_kernel, each), [VMEM] * 4, shape((dw_kernel.shape[0] + 4, chans), f32), [], VMEM
    )(parts, gain, shift, scale)
    return vis, tile_grads.reshape(tile_features.shape), param_grads


def solution(mesh):
    grid = Mesh(mesh.devices.reshape(4, 4, 4, 4, 2), DP + ENC)
    placed = (
        P(DP, None, None, ENC),
        P(None, ENC),
        P(ENC),
        P(ENC),
        P(ENC),
        P(ENC),
        P(DP, None),
        P(DP, None),
        P(DP, None),
        P(DP, ENC),
    )
    return jax.shard_map(
        per_device,
        mesh=grid,
        in_specs=placed,
        out_specs=(P(DP, ENC), P(DP, None, None, ENC), P(None, ENC)),
        check_vma=False,
    )
```
